32 devices in a mesh: groups: 2 (over x), dp: 8 (over z, y), tensor: 2 (over core).
Axes of the slice: x: 2, y: 2, z: 4, core: 2. Of those that a mesh axis runs over, the one named last changes fastest.
Arguments:
- queries: bfloat16 [2048, 8192], P(('groups', 'dp'), 'tensor'), parts along dimension 0
- response_key_rows: bfloat16 [2048, 1024], P(('groups', 'dp'), 'tensor'), parts along dimension 0
- response_value_rows: bfloat16 [2048, 1024], P(('groups', 'dp'), 'tensor'), parts along dimension 0, may hold values from -6 to 6
- shared_prompt_keys: bfloat16 [16, 768, 1024], P(('groups', 'dp'), None, 'tensor'), parts along dimension 0, may hold values from -6 to 6
- shared_prompt_values: bfloat16 [16, 768, 1024], P(('groups', 'dp'), None, 'tensor'), parts along dimension 0, may hold values from -6 to 6
- grad_out: bfloat16 [2048, 8192], P(('groups', 'dp'), 'tensor'), parts along dimension 0, may hold values from -6 to 6
- lengths: int32 [64], P('groups'), parts along dimension 0, may hold values from 1 to 64, as said below
- packing: int32 [16, 6], P(('groups', 'dp')), parts along dimension 0, may hold values from -1 to 31, as said below
- prompt_of: int32 [64], P('groups'), parts along dimension 0, may hold values from 0 to 7, as said below
- prompt_owner: int32 [16], P('groups'), parts along dimension 0, may hold values from 0 to 7, as said below
Outputs:
- attn_out: bfloat16 [2048, 8192], P(('groups', 'dp'), 'tensor'), parts along dimension 0
- grad_queries: bfloat16 [2048, 8192], P(('groups', 'dp'), 'tensor'), parts along dimension 0
- grad_response_keys: bfloat16 [2048, 1024], P(('groups', 'dp'), 'tensor'), parts along dimension 0
- grad_response_values: bfloat16 [2048, 1024], P(('groups', 'dp'), 'tensor'), parts along dimension 0
- grad_prompt_keys: bfloat16 [16, 768, 1024], P(('groups', 'dp'), None, 'tensor'), parts along dimension 0
- grad_prompt_values: bfloat16 [16, 768, 1024], P(('groups', 'dp'), None, 'tensor'), parts along dimension 0
The draws below stay inside these ranges and needn't reach their ends.
There are 2 independent parts, one for each index of `groups`. The reference program is written for one: setup_inputs(seed, part) draws one part's arguments, and reference() takes and returns one part's arrays. A program takes and returns all parts, laid end to end along the dimension named above; each array names one. Nothing has to cross between parts.
Inputs may be any that keep to these rules, and one draw needn't show every extreme that they name: `prompt_of`: each prompt has exactly 4 responses. A permutation: prompt p sits at slot prompt_owner[p] of shared_prompt_keys and shared_prompt_values. `packing`: every response is named in exactly one list. List b names responses of the prompt at slot b first, then responses of the prompt at slot (b - 1) mod 8, then -1 entries; it names at least 2 responses. `lengths`: the responses of one list have 128 tokens or fewer together; some response has 64 tokens.
All inputs are finite; a program needn't handle non-finite values.
Results may differ from the reference program's by a relative error of at most 0.0035.
The reference program's roundings to bfloat16 on the way (of `attention_low`, `grad_live` and `grad_scores`) count: a program that leaves them out, or rounds other values in their place, can miss the bound.
Values may be sent and summed in bfloat16 or wider, within the bound.
No kernel may reach another device: no remote copies, remote signals or barrier semaphores. Data moves between devices by JAX's collectives and lax.ppermute only.
A program may use at most 64 MiB of HBM per device.

```python
import jax
import jax.numpy as jnp
from jax import lax

QUERY_HEAD_COUNT = 64
KEY_VALUE_HEADS = 8
HEAD_WIDTH = 128
PROMPT_LENGTH = 768
TOKEN_ROWS_LOCAL = 128
GROUP = 4
SLOTS = 6
PROMPT_COUNT = 8
RESP = 32
RESPONSE_ROWS = 1024
N_DP = 8


def packing_plan(key):
    plan_key = jax.random.fold_in(key, 101)
    owner_key, order_key, spill_key, length_key = jax.random.split(plan_key, 4)
    prompt_owner = jax.random.permutation(owner_key, PROMPT_COUNT).astype(jnp.int32)
    shuffled = jax.random.permutation(order_key, RESP).astype(jnp.int32)
    prompt_of = (shuffled // GROUP).astype(jnp.int32)
    members = jnp.argsort(shuffled).astype(jnp.int32).reshape(PROMPT_COUNT, GROUP)
    spills = jax.random.randint(spill_key, (N_DP,), 1, GROUP).astype(jnp.int32)
    spills = spills.at[0].set(GROUP - 1).at[N_DP - 1].set(1)
    owned = jnp.argsort(prompt_owner).astype(jnp.int32)
    kept = GROUP - spills
    arrived = jnp.roll(spills, 1)
    own_lists = members[owned]
    left_lists = jnp.roll(own_lists, 1, axis=0)
    slot_index = jnp.broadcast_to(jnp.arange(SLOTS, dtype=jnp.int32)[None, :], (N_DP, SLOTS))
    own_pick = jnp.take_along_axis(own_lists, jnp.minimum(slot_index, GROUP - 1), axis=1)
    offset = slot_index - kept[:, None]
    left_pick = jnp.take_along_axis(left_lists, jnp.clip(GROUP - arrived[:, None] + offset, 0, GROUP - 1), axis=1)
    packing = jnp.where(slot_index < kept[:, None], own_pick, jnp.where((offset >= 0) & (offset < arrived[:, None]), left_pick, -1)).astype(jnp.int32)
    counts = kept + arrived
    holder = prompt_owner[prompt_of]
    position = shuffled % GROUP
    home_row = jnp.where(position < kept[holder], holder, (holder + 1) % N_DP)
    limit = TOKEN_ROWS_LOCAL // counts[home_row]
    drawn_sample = jax.random.randint(length_key, (RESP,), 1, limit + 1).astype(jnp.int32)
    lengths = jnp.where(home_row == 0, limit, drawn_sample).astype(jnp.int32)
    return (prompt_owner, prompt_of, packing, lengths)


def draw_lengths(key, part):
    shared = packing_plan(key)
    return shared[3]


def draw_packing(key, part):
    shared = packing_plan(key)
    return shared[2]


def draw_prompt_of(key, part):
    shared = packing_plan(key)
    return shared[1]


def draw_prompt_owner(key, part):
    shared = packing_plan(key)
    return shared[0]


def draw_queries(key, part):
    key = jax.random.fold_in(key, 5)
    drawn_sample = jnp.clip(1.5 * jax.random.normal(key, (RESPONSE_ROWS, QUERY_HEAD_COUNT * HEAD_WIDTH), jnp.float32), -9.0, 9.0)
    return drawn_sample.astype(jnp.bfloat16)


def draw_response_key_rows(key, part):
    key = jax.random.fold_in(key, 6)
    drawn_sample = jnp.clip(jax.random.normal(key, (RESPONSE_ROWS, KEY_VALUE_HEADS * HEAD_WIDTH), jnp.float32), -6.0, 6.0)
    return drawn_sample.astype(jnp.bfloat16)


def block_scale(rng, shape, pieces, low, high):
    def one(dim, blocks):
        steps = jax.random.uniform(jax.random.fold_in(jax.random.fold_in(rng, 6), dim), (blocks,), jnp.float32, low / len(pieces), high / len(pieces))
        return jnp.repeat(jnp.exp(steps), shape[dim] // blocks).reshape((-1,) + (1,) * (len(shape) - dim - 1))

    loudness = one(*pieces[0])
    for cut in pieces[1:]:
        loudness = loudness * one(*cut)
    return loudness


def normal_values(key, extent, deviation, reach, cuts=(), kind=jnp.bfloat16):
    gain = block_scale(key, extent, cuts, -0.22, 0.18) if cuts else 1.0
    values = jax.random.normal(key, extent, jnp.float32) * deviation * gain
    return jnp.minimum(jnp.maximum(values, -reach), reach).astype(kind)


def setup_inputs(seed: int = 0, part: int = 0) -> dict:
    key_list = jax.random.split(jax.random.key(seed), 11)
    part_splits = jax.random.split(jax.random.fold_in(key_list[10], part), 11)
    return {
        "queries": draw_queries(jax.random.fold_in(jax.random.fold_in(key_list[10], part), 71), part),
        "response_key_rows": draw_response_key_rows(jax.random.fold_in(jax.random.fold_in(key_list[10], part), 71), part),
        "response_value_rows": normal_values(part_splits[2], (RESPONSE_ROWS, KEY_VALUE_HEADS * HEAD_WIDTH), 1.0, 6.0, ((0, 8), (1, 2))),
        "shared_prompt_keys": normal_values(part_splits[3], (PROMPT_COUNT, PROMPT_LENGTH, KEY_VALUE_HEADS * HEAD_WIDTH), 1.0, 6.0, ((0, 8), (2, 2))),
        "shared_prompt_values": normal_values(part_splits[4], (PROMPT_COUNT, PROMPT_LENGTH, KEY_VALUE_HEADS * HEAD_WIDTH), 1.0, 6.0, ((0, 8), (2, 2))),
        "grad_out": normal_values(part_splits[5], (RESPONSE_ROWS, QUERY_HEAD_COUNT * HEAD_WIDTH), 1.0, 6.0, ((0, 8), (1, 2))),
        "lengths": draw_lengths(jax.random.fold_in(jax.random.fold_in(key_list[10], part), 71), part),
        "packing": draw_packing(jax.random.fold_in(jax.random.fold_in(key_list[10], part), 71), part),
        "prompt_of": draw_prompt_of(jax.random.fold_in(jax.random.fold_in(key_list[10], part), 71), part),
        "prompt_owner": draw_prompt_owner(jax.random.fold_in(jax.random.fold_in(key_list[10], part), 71), part),
    }


NEGATIVE = -1e30


def layout(entries, lengths, prompt_of, prompt_owner, device, devices, rows_here, prompt_len):
    lookup = jnp.arange(lengths.shape[0], dtype=jnp.int32)
    chosen = entries[:, None] == lookup[None, :]
    span_lengths = jnp.sum(jnp.where(chosen, lengths[None, :], 0), axis=1).astype(jnp.int32)
    prompts_here = jnp.sum(jnp.where(chosen, prompt_of[None, :], 0), axis=1).astype(jnp.int32)
    prompt_lookup = jnp.arange(prompt_owner.shape[0], dtype=jnp.int32)
    holders = jnp.sum(jnp.where(prompts_here[:, None] == prompt_lookup[None, :], prompt_owner[None, :], 0), axis=1).astype(jnp.int32)
    row_ends = jnp.cumsum(span_lengths).astype(jnp.int32)
    row_starts = row_ends - span_lengths
    row_index = jnp.arange(rows_here, dtype=jnp.int32)
    inside = (row_index[:, None] >= row_starts[None, :]) & (row_index[:, None] < row_ends[None, :])
    live_rows = jnp.any(inside, axis=1)
    slot_index = jnp.arange(entries.shape[0], dtype=jnp.int32)
    slot_of = jnp.where(live_rows, jnp.sum(jnp.where(inside, slot_index[None, :], 0), axis=1), -1).astype(jnp.int32)
    own_rows = jnp.any(inside & (holders == device)[None, :], axis=1)
    left_rows = jnp.any(inside & (holders == (device + devices - 1) % devices)[None, :], axis=1)
    causal = (slot_of[:, None] == slot_of[None, :]) & live_rows[:, None] & (row_index[None, :] <= row_index[:, None])
    local_cols = causal | (row_index[:, None] == row_index[None, :])
    own_cols = jnp.broadcast_to(own_rows[:, None], (rows_here, prompt_len))
    left_cols = jnp.broadcast_to(left_rows[:, None], (rows_here, prompt_len))
    return own_cols, left_cols, local_cols, live_rows


def attend_all(query_rows, context_keys, context_values, grad_rows, allowed, live_rows):
    rows_here = query_rows.shape[0]
    kv_heads = context_keys.shape[1]
    group_size = query_rows.shape[1] // kv_heads
    score_scale = HEAD_WIDTH ** -0.5
    query_f = query_rows.reshape(rows_here, kv_heads, group_size, HEAD_WIDTH).astype(jnp.float32)
    key_f = context_keys.astype(jnp.float32)
    value_f = context_values.astype(jnp.float32)
    scores = jnp.einsum("tkgd,skd->kgts", query_f, key_f) * score_scale
    scores = jnp.where(allowed[None, None], scores, NEGATIVE)
    row_max = jnp.max(scores, axis=-1, keepdims=True)
    exponent = jnp.exp(scores - row_max)
    row_sum = jnp.sum(exponent, axis=-1, keepdims=True)
    attention = exponent / row_sum
    attention_low = lax.optimization_barrier(attention.astype(jnp.bfloat16)).astype(jnp.float32)
    weighted = jnp.einsum("kgts,skd->tkgd", attention_low, value_f)
    live_mask = live_rows[:, None, None, None]
    result = jnp.where(live_mask, weighted, 0.0).astype(jnp.bfloat16)
    grad_live = jnp.where(live_mask, grad_rows.reshape(rows_here, kv_heads, group_size, HEAD_WIDTH), 0.0).astype(jnp.bfloat16)
    grad_f = grad_live.astype(jnp.float32)
    row_dot = jnp.sum(grad_f * result.astype(jnp.float32), axis=-1)
    grad_attention = jnp.einsum("tkgd,skd->kgts", grad_f, value_f)
    grad_scores = attention * (grad_attention - jnp.transpose(row_dot, (1, 2, 0))[..., None])
    grad_low = lax.optimization_barrier(grad_scores.astype(jnp.bfloat16)).astype(jnp.float32)
    grad_query = score_scale * jnp.einsum("kgts,skd->tkgd", grad_low, key_f)
    grad_key = score_scale * jnp.einsum("kgts,tkgd->skd", grad_low, query_f)
    grad_value = jnp.einsum("kgts,tkgd->skd", attention_low, grad_f)
    return result, grad_query.astype(jnp.bfloat16), grad_key, grad_value


def reference(queries, response_key_rows, response_value_rows, shared_prompt_keys, shared_prompt_values, grad_out, lengths, packing, prompt_of, prompt_owner):
    query_blocks = queries.reshape(N_DP, TOKEN_ROWS_LOCAL, QUERY_HEAD_COUNT, HEAD_WIDTH)
    key_tiles = response_key_rows.reshape(N_DP, TOKEN_ROWS_LOCAL, KEY_VALUE_HEADS, HEAD_WIDTH)
    value_tiles = response_value_rows.reshape(N_DP, TOKEN_ROWS_LOCAL, KEY_VALUE_HEADS, HEAD_WIDTH)
    grad_blocks = grad_out.reshape(N_DP, TOKEN_ROWS_LOCAL, QUERY_HEAD_COUNT, HEAD_WIDTH)
    prompt_key_tiles = shared_prompt_keys.reshape(N_DP, PROMPT_LENGTH, KEY_VALUE_HEADS, HEAD_WIDTH)
    prompt_value_tiles = shared_prompt_values.reshape(N_DP, PROMPT_LENGTH, KEY_VALUE_HEADS, HEAD_WIDTH)
    borrowed_keys = jnp.roll(prompt_key_tiles, 1, axis=0)
    borrowed_values = jnp.roll(prompt_value_tiles, 1, axis=0)
    device_ids = jnp.arange(N_DP, dtype=jnp.int32)

    def per_device(operands):
        device, query_rows, key_rows, value_rows, grad_rows, own_keys, own_values, left_keys, left_values, entries = operands
        own_cols, left_cols, local_cols, live_rows = layout(entries, lengths, prompt_of, prompt_owner, device, N_DP, TOKEN_ROWS_LOCAL, PROMPT_LENGTH)
        allowed = jnp.concatenate([own_cols, left_cols, local_cols], axis=1)
        context_keys = jnp.concatenate([own_keys, left_keys, key_rows], axis=0)
        context_values = jnp.concatenate([own_values, left_values, value_rows], axis=0)
        result, grad_query, grad_key, grad_value = attend_all(query_rows, context_keys, context_values, grad_rows, allowed, live_rows)
        return (result, grad_query, grad_key[2 * PROMPT_LENGTH:].astype(jnp.bfloat16), grad_value[2 * PROMPT_LENGTH:].astype(jnp.bfloat16),
                grad_key[:PROMPT_LENGTH], grad_value[:PROMPT_LENGTH], grad_key[PROMPT_LENGTH:2 * PROMPT_LENGTH], grad_value[PROMPT_LENGTH:2 * PROMPT_LENGTH])

    outputs = lax.map(per_device, (device_ids, query_blocks, key_tiles, value_tiles, grad_blocks,
                                   prompt_key_tiles, prompt_value_tiles, borrowed_keys, borrowed_values, packing))
    result, grad_query, resident_key, resident_value, own_key, own_value, left_key, left_value = outputs
    prompt_key_gradient = (own_key + jnp.roll(left_key, -1, axis=0)).astype(jnp.bfloat16)
    prompt_value_gradient = (own_value + jnp.roll(left_value, -1, axis=0)).astype(jnp.bfloat16)
    return (result.reshape(RESPONSE_ROWS, QUERY_HEAD_COUNT * HEAD_WIDTH), grad_query.reshape(RESPONSE_ROWS, QUERY_HEAD_COUNT * HEAD_WIDTH),
            resident_key.reshape(RESPONSE_ROWS, KEY_VALUE_HEADS * HEAD_WIDTH), resident_value.reshape(RESPONSE_ROWS, KEY_VALUE_HEADS * HEAD_WIDTH),
            prompt_key_gradient.reshape(PROMPT_COUNT, PROMPT_LENGTH, KEY_VALUE_HEADS * HEAD_WIDTH), prompt_value_gradient.reshape(PROMPT_COUNT, PROMPT_LENGTH, KEY_VALUE_HEADS * HEAD_WIDTH))
```

```python
import functools

import jax
import jax.numpy as jnp
from jax import lax
from jax.experimental import pallas as pl
from jax.experimental.pallas import tpu as pltpu
from jax.sharding import PartitionSpec as P

HEAD_WIDTH = 128
TILE_ROWS = 32
SCORE_SCALE = HEAD_WIDTH ** -0.5
LOG2_E = 1.4426950408889634
NEGATIVE = -1e30
F32 = jnp.float32
BF16 = jnp.bfloat16
VMEM_LIMIT = 48 * 1024 * 1024


def shifted(value, axis, steps):
    count = lax.axis_size(axis)
    pairs = [(source, (source + steps) % count) for source in range(count)]
    return lax.ppermute(value, axis, pairs)


def dot(left, right):
    return lax.dot_general(
        left, right, (((1,), (0,)), ((), ())), preferred_element_type=F32
    )


def plan(scalars):
    device, packing, lengths, prompt_of, prompt_owner = scalars
    own = jnp.int32(0)
    total = jnp.int32(0)
    ends = []
    for slot in range(packing.shape[1]):
        entry = packing[0, slot]
        used = entry >= 0
        index = jnp.maximum(entry, 0)
        length = jnp.where(used, lengths[index], 0)
        holder = prompt_owner[prompt_of[index]]
        own = own + jnp.where(holder == device[0], length, 0)
        total = total + length
        ends.append(total)
    return own, total, ends


def tile_of(ref, row, group):
    rows = ref[pl.ds(row, TILE_ROWS), :]
    return jnp.concatenate(
        [rows[:, g * HEAD_WIDTH : (g + 1) * HEAD_WIDTH] for g in range(group)], axis=0
    )


def put_tile(ref, row, group, value):
    for g in range(group):
        ref[pl.ds(row, TILE_ROWS), g * HEAD_WIDTH : (g + 1) * HEAD_WIDTH] = value[
            g * TILE_ROWS : (g + 1) * TILE_ROWS
        ]


def local_mask(first_row, ends, keys, columns):
    column = lax.broadcasted_iota(jnp.int32, (1, columns), 1)
    row = first_row + lax.rem(column, TILE_ROWS)
    start = jnp.zeros((1, columns), jnp.int32)
    for end in ends:
        start = jnp.where(row >= end, end, start)
    key = lax.broadcasted_iota(jnp.int32, (keys, columns), 0)
    return (key >= start) & (key <= row)


def gather_kernel(*refs):
    scalars, (query, grad, rows_out, count_out) = refs[:5], refs[5:]
    own, total, _ = plan(scalars)
    rows = query.shape[0]
    target = lax.broadcasted_iota(jnp.int32, (rows, rows), 0)
    source = lax.broadcasted_iota(jnp.int32, (rows, rows), 1)
    pick = ((source == target + own) & (source < total)).astype(BF16)
    rows_out[0] = dot(pick, query[...]).astype(BF16)
    rows_out[1] = dot(pick, grad[...]).astype(BF16)
    count_out[...] = jnp.full(count_out.shape, total - own, jnp.int32)


def segment(
    count, offset, ends, query_tile, grad_tile, keys, values, local_keys, local_values,
    group, put, key_acc, value_acc, local_key_acc, local_value_acc,
):
    columns = group * TILE_ROWS
    keys_t = keys.T
    values_t = values.T
    local_keys_t = local_keys.T
    local_values_t = local_values.T
    scale2 = SCORE_SCALE * LOG2_E

    def body(tile, carry):
        row = pl.multiple_of(tile * TILE_ROWS, TILE_ROWS)
        within = row + lax.rem(lax.broadcasted_iota(jnp.int32, (columns, 1), 0), TILE_ROWS)
        query = jnp.where(within < count, query_tile(row), 0)
        grad = jnp.where(within < count, grad_tile(row), 0)
        query_t = query.T
        grad_t = grad.T
        within_t = row + lax.rem(lax.broadcasted_iota(jnp.int32, (1, columns), 1), TILE_ROWS)
        allowed = local_mask(row + offset, ends, local_keys.shape[0], columns)
        scores = dot(keys, query_t) * scale2
        local_scores = jnp.where(allowed, dot(local_keys, query_t) * scale2, NEGATIVE)
        top = jnp.maximum(
            jnp.max(scores, axis=0, keepdims=True), jnp.max(local_scores, axis=0, keepdims=True)
        )
        weight = jnp.exp2(scores - top)
        local_weight = jnp.exp2(local_scores - top)
        inverse = 1.0 / (
            jnp.sum(weight, axis=0, keepdims=True) + jnp.sum(local_weight, axis=0, keepdims=True)
        )
        weight = weight * inverse
        local_weight = local_weight * inverse
        weight_low = weight.astype(BF16)
        local_weight_low = local_weight.astype(BF16)
        out_t = dot(values_t, weight_low) + dot(local_values_t, local_weight_low)
        out_t = jnp.where(within_t < count, out_t, 0.0).astype(BF16)
        row_dot = jnp.sum(out_t.astype(F32) * grad_t.astype(F32), axis=0, keepdims=True)
        grad_scores = (weight * (dot(values, grad_t) - row_dot)).astype(BF16)
        local_grad_scores = (local_weight * (dot(local_values, grad_t) - row_dot)).astype(BF16)
        grad_query_t = (
            dot(keys_t, grad_scores) + dot(local_keys_t, local_grad_scores)
        ) * SCORE_SCALE
        if key_acc is not None:
            key_acc[...] += dot(grad_scores, query) * SCORE_SCALE
            value_acc[...] += dot(weight_low, grad)
        local_key_acc[...] += dot(local_grad_scores, query) * SCORE_SCALE
        local_value_acc[...] += dot(local_weight_low, grad)
        put(tile, row, out_t.T, grad_query_t.astype(BF16).T, top, inverse, row_dot)
        return carry

    lax.fori_loop(0, lax.div(count + TILE_ROWS - 1, TILE_ROWS), body, 0)


def own_kernel(*refs):
    scalars = refs[:5]
    (query, grad, keys, values, local_keys, local_values, out, grad_query, local_key, local_value,
     key_part, value_part) = refs[5:]
    own, _, ends = plan(scalars)
    group = query.shape[1] // HEAD_WIDTH
    for ref in (out, grad_query, local_key, local_value, key_part, value_part):
        ref[...] = jnp.zeros(ref.shape, ref.dtype)

    def put(tile, row, out_tile, grad_query_tile, top, inverse, row_dot):
        put_tile(out, row, group, out_tile)
        put_tile(grad_query, row, group, grad_query_tile)

    segment(
        own, 0, ends,
        lambda row: tile_of(query, row, group), lambda row: tile_of(grad, row, group),
        keys[...], values[...], local_keys[...], local_values[...],
        group, put, key_part, value_part, local_key, local_value,
    )


def left_kernel(*refs):
    scalars = refs[:5]
    (rows, keys, values, local_keys, local_values, own_out, own_grad_query, own_local_key,
     own_local_value, out, grad_query, local_key, local_value, stats,
     left_out, left_grad_query, key_acc, value_acc) = refs[5:]
    own, total, ends = plan(scalars)
    head = pl.program_id(0)
    group = rows.shape[2] // HEAD_WIDTH
    columns = group * TILE_ROWS
    count = rows.shape[1]
    left_out[...] = jnp.zeros(left_out.shape, BF16)
    left_grad_query[...] = jnp.zeros(left_grad_query.shape, BF16)
    key_acc[...] = own_local_key[...]
    value_acc[...] = own_local_value[...]

    @pl.when(head == 0)
    def _():
        stats[...] = jnp.zeros(stats.shape, F32)

    def put(tile, row, out_tile, grad_query_tile, top, inverse, row_dot):
        put_tile(left_out, row, group, out_tile)
        put_tile(left_grad_query, row, group, grad_query_tile)
        for index, value in enumerate((top, inverse, row_dot)):
            stats[pl.ds(head * 4 + index, 1), pl.ds(pl.multiple_of(tile * columns, columns), columns)] = value

    segment(
        total - own, own, ends,
        lambda row: tile_of(rows.at[0], row, group), lambda row: tile_of(rows.at[1], row, group),
        keys[...], values[...], local_keys[...], local_values[...],
        group, put, None, None, key_acc, value_acc,
    )
    target = lax.broadcasted_iota(jnp.int32, (count, count), 0)
    source = lax.broadcasted_iota(jnp.int32, (count, count), 1)
    place = (target == source + own).astype(BF16)
    out[...] = (own_out[...].astype(F32) + dot(place, left_out[...])).astype(BF16)
    grad_query[...] = (own_grad_query[...].astype(F32) + dot(place, left_grad_query[...])).astype(BF16)
    local_key[...] = key_acc[...].astype(BF16)
    local_value[...] = value_acc[...].astype(BF16)


def arrived_kernel(count, rows, stats, keys, values, own_key, own_value, key_out, value_out,
                   key_acc, value_acc):
    head = pl.program_id(0)
    group = rows.shape[2] // HEAD_WIDTH
    columns = group * TILE_ROWS
    scale2 = SCORE_SCALE * LOG2_E
    key_acc[...] = own_key[...]
    value_acc[...] = own_value[...]

    def body(tile, carry):
        row = pl.multiple_of(tile * TILE_ROWS, TILE_ROWS)
        query = tile_of(rows.at[0], row, group)
        grad = tile_of(rows.at[1], row, group)
        where = pl.ds(pl.multiple_of(tile * columns, columns), columns)
        top = stats[pl.ds(head * 4, 1), where]
        inverse = stats[pl.ds(head * 4 + 1, 1), where]
        row_dot = stats[pl.ds(head * 4 + 2, 1), where]
        weight = jnp.exp2(dot(keys[...], query.T) * scale2 - top) * inverse
        grad_scores = (weight * (dot(values[...], grad.T) - row_dot)).astype(BF16)
        key_acc[...] += dot(grad_scores, query) * SCORE_SCALE
        value_acc[...] += dot(weight.astype(BF16), grad)
        return carry

    lax.fori_loop(0, lax.div(count[0, 0] + TILE_ROWS - 1, TILE_ROWS), body, 0)
    key_out[0] = key_acc[...].astype(BF16)
    value_out[0] = value_acc[...].astype(BF16)


def per_device(
    queries, response_key_rows, response_value_rows, shared_prompt_keys, shared_prompt_values,
    grad_out, lengths, packing, prompt_of, prompt_owner,
):
    rows = queries.shape[0]
    kv_heads = response_key_rows.shape[1] // HEAD_WIDTH
    width = queries.shape[1] // kv_heads
    prompt = shared_prompt_keys.shape[1]
    device = lax.axis_index("dp").astype(jnp.int32).reshape(1)
    scalars = (device, packing, lengths, prompt_of, prompt_owner)
    smem = [pl.BlockSpec(memory_space=pltpu.SMEM)] * 5
    params = pltpu.CompilerParams(vmem_limit_bytes=VMEM_LIMIT)
    shape = jax.ShapeDtypeStruct
    wide = pl.BlockSpec((rows, width), lambda h: (0, h))
    narrow = pl.BlockSpec((rows, HEAD_WIDTH), lambda h: (0, h))
    context = pl.BlockSpec((prompt, HEAD_WIDTH), lambda h: (0, h))
    pair = pl.BlockSpec((2, rows, width), lambda h: (0, 0, h))
    own_keys = shared_prompt_keys[0]
    own_values = shared_prompt_values[0]
    stat_columns = rows * width // HEAD_WIDTH
    stat_block = pl.BlockSpec((4 * kv_heads, stat_columns), lambda h: (0, 0))

    left_keys = shifted(own_keys, "dp", 1)
    left_values = shifted(own_values, "dp", 1)

    moved, count = pl.pallas_call(
        gather_kernel,
        grid=(kv_heads,),
        in_specs=smem + [wide, wide],
        out_specs=[pair, pl.BlockSpec((8, 128), lambda h: (0, 0))],
        out_shape=[shape((2, rows, queries.shape[1]), BF16), shape((8, 128), jnp.int32)],
        compiler_params=params,
        name="gather_rows",
    )(*scalars, queries, grad_out)
    arrived_count = shifted(count, "dp", -1)
    arrived = shifted(moved, "dp", -1)

    own_out, own_grad_query, own_local_key, own_local_value, own_key, own_value = pl.pallas_call(
        own_kernel,
        grid=(kv_heads,),
        in_specs=smem + [wide, wide, context, context, narrow, narrow],
        out_specs=[wide, wide, narrow, narrow, context, context],
        out_shape=[
            shape(queries.shape, BF16), shape(queries.shape, BF16),
            shape(response_key_rows.shape, F32), shape(response_key_rows.shape, F32),
            shape(own_keys.shape, F32), shape(own_keys.shape, F32),
        ],
        compiler_params=params,
        name="own_rows",
    )(*scalars, queries, grad_out, own_keys, own_values, response_key_rows, response_value_rows)

    out, grad_query, local_key, local_value, stats = pl.pallas_call(
        left_kernel,
        grid=(kv_heads,),
        in_specs=smem + [pair, context, context, narrow, narrow, wide, wide, narrow, narrow],
        out_specs=[wide, wide, narrow, narrow, stat_block],
        out_shape=[
            shape(queries.shape, BF16), shape(queries.shape, BF16),
            shape(response_key_rows.shape, BF16), shape(response_key_rows.shape, BF16),
            shape((4 * kv_heads, stat_columns), F32),
        ],
        scratch_shapes=[
            pltpu.VMEM((rows, width), BF16), pltpu.VMEM((rows, width), BF16),
            pltpu.VMEM((rows, HEAD_WIDTH), F32), pltpu.VMEM((rows, HEAD_WIDTH), F32),
        ],
        compiler_params=params,
        name="left_rows",
    )(*scalars, moved, left_keys, left_values, response_key_rows, response_value_rows,
      own_out, own_grad_query, own_local_key, own_local_value)
    arrived_stats = shifted(stats, "dp", -1)

    whole = pl.BlockSpec((1, prompt, HEAD_WIDTH), lambda h: (0, 0, h))
    prompt_key, prompt_value = pl.pallas_call(
        arrived_kernel,
        grid=(kv_heads,),
        in_specs=[pl.BlockSpec(memory_space=pltpu.SMEM), pair, stat_block, context, context, context, context],
        out_specs=[whole, whole],
        out_shape=[shape((1,) + own_keys.shape, BF16)] * 2,
        scratch_shapes=[pltpu.VMEM((prompt, HEAD_WIDTH), F32)] * 2,
        compiler_params=params,
        name="arrived_rows",
    )(arrived_count, arrived, arrived_stats, own_keys, own_values, own_key, own_value)
    return out, grad_query, local_key, local_value, prompt_key, prompt_value


def solution(mesh):
    rows = P(("groups", "dp"), "tensor")
    prompts = P(("groups", "dp"), None, "tensor")
    in_specs = (
        rows, rows, rows, prompts, prompts, rows,
        P("groups"), P(("groups", "dp"), None), P("groups"), P("groups"),
    )
    out_specs = (rows, rows, rows, rows, prompts, prompts)
    return jax.shard_map(
        per_device, mesh=mesh, in_specs=in_specs, out_specs=out_specs, check_vma=False
    )
```

```python
import functools

import jax
import jax.numpy as jnp
from jax import lax
from jax.experimental import pallas as pl
from jax.experimental.pallas import tpu as pltpu
from jax.sharding import PartitionSpec as P

HEAD_WIDTH = 128
TILE_ROWS = 32
SCORE_SCALE = HEAD_WIDTH ** -0.5
LOG2_E = 1.4426950408889634
NEGATIVE = -1e30
F32 = jnp.float32
BF16 = jnp.bfloat16
VMEM_LIMIT = 60 * 1024 * 1024
KEY_CHUNK = 256


def shifted(value, axis, steps):
    count = lax.axis_size(axis)
    pairs = [(source, (source + steps) % count) for source in range(count)]
    return lax.ppermute(value, axis, pairs)


def dot(left, right):
    return lax.dot_general(
        left, right, (((1,), (0,)), ((), ())), preferred_element_type=F32
    )


def dot_nt(left, right):
    return lax.dot_general(
        left, right, (((1,), (1,)), ((), ())), preferred_element_type=F32
    )


def chunks(length, size):
    return [slice(start, min(start + size, length)) for start in range(0, length, size)]


def plan(scalars):
    device, packing, lengths, prompt_of, prompt_owner = scalars
    own = jnp.int32(0)
    total = jnp.int32(0)
    ends = []
    for slot in range(packing.shape[1]):
        entry = packing[0, slot]
        used = entry >= 0
        index = jnp.maximum(entry, 0)
        length = jnp.where(used, lengths[index], 0)
        holder = prompt_owner[prompt_of[index]]
        own = own + jnp.where(holder == device[0], length, 0)
        total = total + length
        ends.append(total)
    return own, total, ends


def tile_of(ref, row, group):
    rows = ref[pl.ds(row, TILE_ROWS), :]
    return jnp.concatenate(
        [rows[:, g * HEAD_WIDTH : (g + 1) * HEAD_WIDTH] for g in range(group)], axis=0
    )


def put_tile(ref, row, group, value):
    for g in range(group):
        ref[pl.ds(row, TILE_ROWS), g * HEAD_WIDTH : (g + 1) * HEAD_WIDTH] = value[
            g * TILE_ROWS : (g + 1) * TILE_ROWS
        ]


def local_mask(first_row, ends, keys, columns):
    column = lax.broadcasted_iota(jnp.int32, (1, columns), 1)
    row = first_row + lax.rem(column, TILE_ROWS)
    start = jnp.zeros((1, columns), jnp.int32)
    for end in ends:
        start = jnp.where(row >= end, end, start)
    key = lax.broadcasted_iota(jnp.int32, (keys, columns), 0)
    return (key >= start) & (key <= row)


def gather_kernel(*refs):
    scalars, (query, grad, moved_out, low_out, high_out, late_out, counts_out) = refs[:5], refs[5:]
    own, total, _ = plan(scalars)
    device, _, lengths, prompt_of, prompt_owner = scalars

    def add(response, sum_of_mine):
        mine = prompt_owner[prompt_of[response]] == device[0]
        return sum_of_mine + jnp.where(mine, lengths[response], 0)

    counts_out[0] = total - own
    counts_out[1] = lax.fori_loop(0, lengths.shape[0], add, jnp.int32(0)) - own
    rows = query.shape[0]
    half, split = rows // 2, low_out.shape[2]
    target = lax.broadcasted_iota(jnp.int32, (rows, rows), 0)
    source = lax.broadcasted_iota(jnp.int32, (rows, rows), 1)
    pick = ((source == target + own) & (source < total)).astype(BF16)
    for index, ref in enumerate((query, grad)):
        picked = dot(pick, ref[...]).astype(BF16)
        moved_out[index] = picked
        low_out[index] = picked[:half, :split]
        high_out[index] = picked[:half, split:]
        late_out[index] = picked[half:]


def segment(
    count, offset, ends, query_tile, grad_tile, keys, values, local_keys, local_values,
    group, put, key_acc, value_acc, local_key_acc, local_value_acc,
):
    columns = group * TILE_ROWS
    keys_t = keys.T
    values_t = values.T
    local_keys_t = local_keys.T
    local_values_t = local_values.T
    scale2 = SCORE_SCALE * LOG2_E

    def body(tile, carry):
        row = pl.multiple_of(tile * TILE_ROWS, TILE_ROWS)
        within = row + lax.rem(lax.broadcasted_iota(jnp.int32, (columns, 1), 0), TILE_ROWS)
        query = jnp.where(within < count, query_tile(row), 0)
        grad = jnp.where(within < count, grad_tile(row), 0)
        query_t = query.T
        grad_t = grad.T
        within_t = row + lax.rem(lax.broadcasted_iota(jnp.int32, (1, columns), 1), TILE_ROWS)
        allowed = local_mask(row + offset, ends, local_keys.shape[0], columns)
        scores = dot(keys, query_t) * scale2
        local_scores = jnp.where(allowed, dot(local_keys, query_t) * scale2, NEGATIVE)
        top = jnp.maximum(
            jnp.max(scores, axis=0, keepdims=True), jnp.max(local_scores, axis=0, keepdims=True)
        )
        weight = jnp.exp2(scores - top)
        local_weight = jnp.exp2(local_scores - top)
        inverse = 1.0 / (
            jnp.sum(weight, axis=0, keepdims=True) + jnp.sum(local_weight, axis=0, keepdims=True)
        )
        weight = weight * inverse
        local_weight = local_weight * inverse
        weight_low = weight.astype(BF16)
        local_weight_low = local_weight.astype(BF16)
        out_t = dot(values_t, weight_low) + dot(local_values_t, local_weight_low)
        out_t = jnp.where(within_t < count, out_t, 0.0).astype(BF16)
        row_dot = jnp.sum(out_t.astype(F32) * grad_t.astype(F32), axis=0, keepdims=True)
        grad_scores = (weight * (dot(values, grad_t) - row_dot)).astype(BF16)
        local_grad_scores = (local_weight * (dot(local_values, grad_t) - row_dot)).astype(BF16)
        grad_query_t = (
            dot(keys_t, grad_scores) + dot(local_keys_t, local_grad_scores)
        ) * SCORE_SCALE
        if key_acc is not None:
            key_acc[...] += dot(grad_scores, query)
            value_acc[...] += dot(weight_low, grad)
        local_key_acc[...] += dot(local_grad_scores, query) * SCORE_SCALE
        local_value_acc[...] += dot(local_weight_low, grad)
        put(tile, row, out_t.T, grad_query_t.astype(BF16).T, top, inverse, row_dot)
        return carry

    lax.fori_loop(0, lax.div(count + TILE_ROWS - 1, TILE_ROWS), body, 0)


def own_kernel(*refs):
    scalars = refs[:5]
    (query, grad, keys, values, local_keys, local_values, out, grad_query, local_key, local_value,
     key_part, value_part) = refs[5:]
    own, _, ends = plan(scalars)
    group = query.shape[1] // HEAD_WIDTH
    for ref in (out, grad_query, local_key, local_value, key_part, value_part):
        ref[...] = jnp.zeros(ref.shape, ref.dtype)

    def put(tile, row, out_tile, grad_query_tile, top, inverse, row_dot):
        put_tile(out, row, group, out_tile)
        put_tile(grad_query, row, group, grad_query_tile)

    segment(
        own, 0, ends,
        lambda row: tile_of(query, row, group), lambda row: tile_of(grad, row, group),
        keys[...], values[...], local_keys[...], local_values[...],
        group, put, key_part, value_part, local_key, local_value,
    )


def left_kernel(*refs):
    scalars = refs[:5]
    (rows, keys, values, local_keys, local_values, own_out, own_grad_query, own_local_key,
     own_local_value, out, grad_query, local_key, local_value, stats,
     left_out, left_grad_query, key_acc, value_acc) = refs[5:]
    own, total, ends = plan(scalars)
    count = total - own
    head = pl.program_id(0)
    group = rows.shape[2] // HEAD_WIDTH
    columns = group * TILE_ROWS
    all_rows = out.shape[0]
    left_out[...] = jnp.zeros(left_out.shape, BF16)
    left_grad_query[...] = jnp.zeros(left_grad_query.shape, BF16)
    key_acc[...] = own_local_key[...]
    value_acc[...] = own_local_value[...]

    @pl.when(head == 0)
    def _():
        stats[...] = jnp.zeros(stats.shape, F32)

    scale2 = SCORE_SCALE * LOG2_E
    parts = chunks(keys.shape[0], KEY_CHUNK)

    def body(tile, carry):
        row = pl.multiple_of(tile * TILE_ROWS, TILE_ROWS)
        query = tile_of(rows.at[0], row, group)
        grad = tile_of(rows.at[1], row, group)
        within = row + lax.rem(lax.broadcasted_iota(jnp.int32, (columns, 1), 0), TILE_ROWS)
        place = within + own
        start = jnp.zeros((columns, 1), jnp.int32)
        for end in ends:
            start = jnp.where(place >= end, end, start)
        key = lax.broadcasted_iota(jnp.int32, (columns, all_rows), 1)
        allowed = (key >= start) & (key <= place)
        scores = [dot_nt(query, keys[part, :]) * scale2 for part in parts]
        scores.append(jnp.where(allowed, dot_nt(query, local_keys[...]) * scale2, NEGATIVE))
        top = functools.reduce(
            jnp.maximum, [jnp.max(score, axis=1, keepdims=True) for score in scores]
        )
        weights = [jnp.exp2(score - top) for score in scores]
        inverse = 1.0 / sum(jnp.sum(weight, axis=1, keepdims=True) for weight in weights)
        weights = [weight * inverse for weight in weights]
        low = [weight.astype(BF16) for weight in weights]
        value_parts = [values[part, :] for part in parts] + [local_values[...]]
        key_parts = [keys[part, :] for part in parts] + [local_keys[...]]
        result = sum(dot(weight, value) for weight, value in zip(low, value_parts))
        result = jnp.where(within < count, result, 0.0).astype(BF16)
        row_dot = jnp.sum(result.astype(F32) * grad.astype(F32), axis=1, keepdims=True)
        grad_scores = [
            (weight * (dot_nt(grad, value) - row_dot)).astype(BF16)
            for weight, value in zip(weights, value_parts)
        ]
        grad_rows = sum(dot(score, part) for score, part in zip(grad_scores, key_parts))
        put_tile(left_out, row, group, result)
        put_tile(left_grad_query, row, group, (grad_rows * SCORE_SCALE).astype(BF16))
        key_acc[...] += dot(grad_scores[-1].T, query) * SCORE_SCALE
        value_acc[...] += dot(low[-1].T, grad)
        lane = lax.broadcasted_iota(jnp.int32, (columns, HEAD_WIDTH), 1)
        packed = jnp.where(lane == 0, top, jnp.where(lane == 1, inverse, row_dot)).T
        where = pl.ds(pl.multiple_of(tile * columns, columns), columns)
        stats[pl.ds(pl.multiple_of(head * 8, 8), 8), where] = packed[:8]
        return carry

    lax.fori_loop(0, lax.div(count + TILE_ROWS - 1, TILE_ROWS), body, 0)
    target = lax.broadcasted_iota(jnp.int32, (all_rows, all_rows), 0)
    source = lax.broadcasted_iota(jnp.int32, (all_rows, all_rows), 1)
    place = (target == source + own).astype(BF16)
    out[...] = (own_out[...].astype(F32) + dot(place, left_out[...])).astype(BF16)
    grad_query[...] = (own_grad_query[...].astype(F32) + dot(place, left_grad_query[...])).astype(BF16)
    local_key[...] = key_acc[...].astype(BF16)
    local_value[...] = value_acc[...].astype(BF16)


def arrived_kernel(first_head, counts, first, second, stats, keys, values, own_key, own_value, *rest):
    key_out, value_out, key_acc, value_acc = rest[-4:]
    head = first_head + pl.program_id(0)
    count = counts[1]
    group = first.shape[2] // HEAD_WIDTH
    columns = group * TILE_ROWS
    scale2 = SCORE_SCALE * LOG2_E
    key_acc[...] = own_key[...]
    value_acc[...] = own_value[...]

    parts = chunks(keys.shape[0], KEY_CHUNK)

    def steps(rows, first_tile):
        def body(tile, carry):
            row = pl.multiple_of(tile * TILE_ROWS, TILE_ROWS)
            within = first_tile * TILE_ROWS + row + lax.rem(
                lax.broadcasted_iota(jnp.int32, (columns, 1), 0), TILE_ROWS
            )
            query = jnp.where(within < count, tile_of(rows.at[0], row, group), 0)
            grad = jnp.where(within < count, tile_of(rows.at[1], row, group), 0)
            where = pl.ds(pl.multiple_of((first_tile + tile) * columns, columns), columns)
            stat = stats[pl.ds(pl.multiple_of(head * 8, 8), 8), where]
            top, inverse, row_dot = stat[0:1], stat[1:2], stat[2:3]
            for part in parts:
                weight = jnp.exp2(dot_nt(keys[part, :], query) * scale2 - top) * inverse
                grad_scores = (weight * (dot_nt(values[part, :], grad) - row_dot)).astype(BF16)
                key_acc[part, :] += dot(grad_scores, query)
                value_acc[part, :] += dot(weight.astype(BF16), grad)
            return carry

        return body

    tiles = lax.div(count + TILE_ROWS - 1, TILE_ROWS)
    full = first.shape[1] // TILE_ROWS
    lax.fori_loop(0, jnp.minimum(tiles, full), steps(first, 0), 0)
    lax.fori_loop(0, jnp.maximum(tiles - full, 0), steps(second, full), 0)
    key_out[0] = (key_acc[...] * SCORE_SCALE).astype(BF16)
    value_out[0] = value_acc[...].astype(BF16)


def after(values, others):
    count = len(values)
    return pl.pallas_call(
        lambda *refs: None,
        in_specs=[pl.BlockSpec(memory_space=pl.ANY)] * (count + len(others)),
        out_specs=[pl.BlockSpec(memory_space=pl.ANY)] * count,
        out_shape=[jax.ShapeDtypeStruct(value.shape, value.dtype) for value in values],
        input_output_aliases={k: k for k in range(count)},
        name="after",
    )(*values, *others)


def send_late(late, send_count, receive_count, device):
    devices = lax.axis_size("dp")
    half = late.shape[1]
    if devices % 2:
        return shifted(late, "dp", -1)
    sizes = [size for size in (0, 8, 16, 32) if size < half] + [half]
    even = lax.rem(device, 2) == 0

    def branch(pairs, receives, size):
        def send(value, received):
            if size == 0:
                return received
            got = lax.ppermute(value[:, :size], "dp", pairs)
            got = jnp.pad(got, ((0, 0), (0, half - size), (0, 0)))
            return jnp.where(receives, got, received)

        return send

    received = late
    for parity in range(2):
        pairs = [(b, (b - 1) % devices) for b in range(parity, devices, 2)]
        sends = even == (parity == 0)
        count = jnp.where(sends, send_count, receive_count)
        choice = sum((count > half + size).astype(jnp.int32) for size in sizes[:-1])
        branches = [branch(pairs, jnp.logical_not(sends), size) for size in sizes]
        received = lax.switch(choice, branches, late, received)
    return received


def per_device(
    queries, response_key_rows, response_value_rows, shared_prompt_keys, shared_prompt_values,
    grad_out, lengths, packing, prompt_of, prompt_owner,
):
    rows = queries.shape[0]
    kv_heads = response_key_rows.shape[1] // HEAD_WIDTH
    width = queries.shape[1] // kv_heads
    prompt = shared_prompt_keys.shape[1]
    device = lax.axis_index("dp").astype(jnp.int32).reshape(1)
    scalars = (device, packing, lengths, prompt_of, prompt_owner)
    smem = [pl.BlockSpec(memory_space=pltpu.SMEM)] * 5
    params = pltpu.CompilerParams(vmem_limit_bytes=VMEM_LIMIT)
    cost = pl.CostEstimate(flops=1, bytes_accessed=1, transcendentals=0)
    shape = jax.ShapeDtypeStruct
    wide = pl.BlockSpec((rows, width), lambda h: (0, h))
    narrow = pl.BlockSpec((rows, HEAD_WIDTH), lambda h: (0, h))
    context = pl.BlockSpec((prompt, HEAD_WIDTH), lambda h: (0, h))
    pair = pl.BlockSpec((2, rows, width), lambda h: (0, 0, h))
    own_keys = shared_prompt_keys[0]
    own_values = shared_prompt_values[0]
    stat_columns = rows * width // HEAD_WIDTH
    stat_block = pl.BlockSpec((8 * kv_heads, stat_columns), lambda h: (0, 0))

    left_keys = shifted(own_keys, "dp", 1)
    left_values = shifted(own_values, "dp", 1)

    half = rows // 2
    low_heads = kv_heads // 2
    split = low_heads * width
    moved, low, high, late, counts = pl.pallas_call(
        gather_kernel,
        in_specs=smem + [pl.BlockSpec(memory_space=pltpu.VMEM)] * 2,
        out_specs=[pl.BlockSpec(memory_space=pltpu.VMEM)] * 4 + [pl.BlockSpec(memory_space=pltpu.SMEM)],
        out_shape=[
            shape((2, rows, queries.shape[1]), BF16),
            shape((2, half, split), BF16), shape((2, half, queries.shape[1] - split), BF16),
            shape((2, half, queries.shape[1]), BF16), shape((2,), jnp.int32),
        ],
        compiler_params=params,
        cost_estimate=cost,
        name="gather_rows",
    )(*scalars, queries, grad_out)

    own_out, own_grad_query, own_local_key, own_local_value, own_key, own_value = pl.pallas_call(
        own_kernel,
        grid=(kv_heads,),
        in_specs=smem + [wide, wide, context, context, narrow, narrow],
        out_specs=[wide, wide, narrow, narrow, context, context],
        out_shape=[
            shape(queries.shape, BF16), shape(queries.shape, BF16),
            shape(response_key_rows.shape, F32), shape(response_key_rows.shape, F32),
            shape(own_keys.shape, F32), shape(own_keys.shape, F32),
        ],
        compiler_params=params,
        cost_estimate=cost,
        name="own_rows",
    )(*scalars, queries, grad_out, own_keys, own_values, response_key_rows, response_value_rows)

    low, late = after((low, late), (own_out,))
    arrived_second = send_late(late, counts[0], counts[1], device[0])
    high, left_values = after((high, left_values), (left_keys, arrived_second))
    arrived_first = [shifted(low, "dp", -1), shifted(high, "dp", -1)]

    out, grad_query, local_key, local_value, stats = pl.pallas_call(
        left_kernel,
        grid=(kv_heads,),
        in_specs=smem + [pair, context, context, narrow, narrow, wide, wide, narrow, narrow],
        out_specs=[wide, wide, narrow, narrow, stat_block],
        out_shape=[
            shape(queries.shape, BF16), shape(queries.shape, BF16),
            shape(response_key_rows.shape, BF16), shape(response_key_rows.shape, BF16),
            shape((8 * kv_heads, stat_columns), F32),
        ],
        scratch_shapes=[
            pltpu.VMEM((rows, width), BF16), pltpu.VMEM((rows, width), BF16),
            pltpu.VMEM((rows, HEAD_WIDTH), F32), pltpu.VMEM((rows, HEAD_WIDTH), F32),
        ],
        compiler_params=params,
        cost_estimate=cost,
        name="left_rows",
    )(*scalars, moved, left_keys, left_values, response_key_rows, response_value_rows,
      own_out, own_grad_query, own_local_key, own_local_value)
    arrived_stats = shifted(stats, "dp", -1)

    outputs = ()
    for part, (start, heads) in enumerate(((0, low_heads), (low_heads, kv_heads - low_heads))):
        here = pl.BlockSpec((prompt, HEAD_WIDTH), lambda h, start=start: (0, h + start))
        first_rows = pl.BlockSpec((2, half, width), lambda h: (0, 0, h))
        second_rows = pl.BlockSpec((2, half, width), lambda h, start=start: (0, 0, h + start))
        whole = pl.BlockSpec((1, prompt, HEAD_WIDTH), lambda h, start=start: (0, 0, h + start))
        outputs = pl.pallas_call(
            functools.partial(arrived_kernel, start),
            grid=(heads,),
            in_specs=[pl.BlockSpec(memory_space=pltpu.SMEM), first_rows, second_rows, stat_block]
            + [here] * 4 + [pl.BlockSpec(memory_space=pl.ANY)] * len(outputs),
            out_specs=[whole, whole],
            out_shape=[shape((1,) + own_keys.shape, BF16)] * 2,
            scratch_shapes=[pltpu.VMEM((prompt, HEAD_WIDTH), F32)] * 2,
            input_output_aliases={8 + k: k for k in range(len(outputs))},
            compiler_params=params,
            cost_estimate=cost,
            name="arrived_rows",
        )(counts, arrived_first[part], arrived_second, arrived_stats, own_keys, own_values,
          own_key, own_value, *outputs)
    prompt_key, prompt_value = outputs
    return out, grad_query, local_key, local_value, prompt_key, prompt_value


def solution(mesh):
    rows = P(("groups", "dp"), "tensor")
    prompts = P(("groups", "dp"), None, "tensor")
    in_specs = (
        rows, rows, rows, prompts, prompts, rows,
        P("groups"), P(("groups", "dp"), None), P("groups"), P("groups"),
    )
    out_specs = (rows, rows, rows, rows, prompts, prompts)
    return jax.shard_map(
        per_device, mesh=mesh, in_specs=in_specs, out_specs=out_specs, check_vma=False
    )
```

```python
import functools

import jax
import jax.numpy as jnp
from jax import lax
from jax.experimental import pallas as pl
from jax.experimental.pallas import tpu as pltpu
from jax.sharding import PartitionSpec as P

HEAD_WIDTH = 128
TILE_ROWS = 32
SCORE_SCALE = HEAD_WIDTH ** -0.5
LOG2_E = 1.4426950408889634
NEGATIVE = -1e30
F32 = jnp.float32
BF16 = jnp.bfloat16
VMEM_LIMIT = 60 * 1024 * 1024
KEY_CHUNK = 256
ARRIVED_CHUNK = 768


def shifted(value, axis, steps):
    count = lax.axis_size(axis)
    pairs = [(source, (source + steps) % count) for source in range(count)]
    return lax.ppermute(value, axis, pairs)


def dot(left, right):
    return lax.dot_general(
        left, right, (((1,), (0,)), ((), ())), preferred_element_type=F32
    )


def dot_nt(left, right):
    return lax.dot_general(
        left, right, (((1,), (1,)), ((), ())), preferred_element_type=F32
    )


def chunks(length, size):
    return [slice(start, min(start + size, length)) for start in range(0, length, size)]


def plan(scalars):
    device, packing, lengths, prompt_of, prompt_owner = scalars
    own = jnp.int32(0)
    total = jnp.int32(0)
    ends = []
    for slot in range(packing.shape[1]):
        entry = packing[0, slot]
        used = entry >= 0
        index = jnp.maximum(entry, 0)
        length = jnp.where(used, lengths[index], 0)
        holder = prompt_owner[prompt_of[index]]
        own = own + jnp.where(holder == device[0], length, 0)
        total = total + length
        ends.append(total)
    return own, total, ends


def tile_of(ref, row, group, first=0):
    columns = [slice(first + g * HEAD_WIDTH, first + (g + 1) * HEAD_WIDTH) for g in range(group)]
    return jnp.concatenate([ref[pl.ds(row, TILE_ROWS), part] for part in columns], axis=0)


def put_tile(ref, row, group, value, first=0):
    for g in range(group):
        columns = slice(first + g * HEAD_WIDTH, first + (g + 1) * HEAD_WIDTH)
        ref[pl.ds(row, TILE_ROWS), columns] = value[g * TILE_ROWS : (g + 1) * TILE_ROWS]


def local_mask(first_row, ends, keys, columns):
    column = lax.broadcasted_iota(jnp.int32, (1, columns), 1)
    row = first_row + lax.rem(column, TILE_ROWS)
    start = jnp.zeros((1, columns), jnp.int32)
    for end in ends:
        start = jnp.where(row >= end, end, start)
    key = lax.broadcasted_iota(jnp.int32, (keys, columns), 0)
    return (key >= start) & (key <= row)


def gather_kernel(*refs):
    scalars = refs[:5]
    query, grad, moved_out, early_out, late_out, counts_out = refs[5:]
    own, total, _ = plan(scalars)
    device, _, lengths, prompt_of, prompt_owner = scalars

    def add(response, sum_of_mine):
        mine = prompt_owner[prompt_of[response]] == device[0]
        return sum_of_mine + jnp.where(mine, lengths[response], 0)

    counts_out[0] = total - own
    counts_out[1] = lax.fori_loop(0, lengths.shape[0], add, jnp.int32(0)) - own
    rows = query.shape[0]
    half = rows // 2
    target = lax.broadcasted_iota(jnp.int32, (rows, rows), 0)
    source = lax.broadcasted_iota(jnp.int32, (rows, rows), 1)
    pick = ((source == target + own) & (source < total)).astype(BF16)
    for index, ref in enumerate((query, grad)):
        picked = dot(pick, ref[...]).astype(BF16)
        moved_out[index] = picked
        early_out[index] = picked[:half]
        late_out[index] = picked[half:]


def segment(
    count, offset, ends, query_tile, grad_tile, keys, values, local_keys, local_values,
    group, put, key_acc, value_acc, local_key_acc, local_value_acc,
):
    columns = group * TILE_ROWS
    keys_t = keys.T
    values_t = values.T
    local_keys_t = local_keys.T
    local_values_t = local_values.T
    scale2 = SCORE_SCALE * LOG2_E

    def body(tile, carry):
        row = pl.multiple_of(tile * TILE_ROWS, TILE_ROWS)
        within = row + lax.rem(lax.broadcasted_iota(jnp.int32, (columns, 1), 0), TILE_ROWS)
        query = jnp.where(within < count, query_tile(row), 0)
        grad = jnp.where(within < count, grad_tile(row), 0)
        query_t = query.T
        grad_t = grad.T
        within_t = row + lax.rem(lax.broadcasted_iota(jnp.int32, (1, columns), 1), TILE_ROWS)
        allowed = local_mask(row + offset, ends, local_keys.shape[0], columns)
        scores = dot(keys, query_t) * scale2
        local_scores = jnp.where(allowed, dot(local_keys, query_t) * scale2, NEGATIVE)
        top = jnp.maximum(
            jnp.max(scores, axis=0, keepdims=True), jnp.max(local_scores, axis=0, keepdims=True)
        )
        weight = jnp.exp2(scores - top)
        local_weight = jnp.exp2(local_scores - top)
        inverse = 1.0 / (
            jnp.sum(weight, axis=0, keepdims=True) + jnp.sum(local_weight, axis=0, keepdims=True)
        )
        weight = weight * inverse
        local_weight = local_weight * inverse
        weight_low = weight.astype(BF16)
        local_weight_low = local_weight.astype(BF16)
        out_t = dot(values_t, weight_low) + dot(local_values_t, local_weight_low)
        out_t = jnp.where(within_t < count, out_t, 0.0).astype(BF16)
        row_dot = jnp.sum(out_t.astype(F32) * grad_t.astype(F32), axis=0, keepdims=True)
        grad_scores = (weight * (dot(values, grad_t) - row_dot)).astype(BF16)
        local_grad_scores = (local_weight * (dot(local_values, grad_t) - row_dot)).astype(BF16)
        grad_query_t = (
            dot(keys_t, grad_scores) + dot(local_keys_t, local_grad_scores)
        ) * SCORE_SCALE
        if key_acc is not None:
            key_acc[...] += dot(grad_scores, query)
            value_acc[...] += dot(weight_low, grad)
        local_key_acc[...] += dot(local_grad_scores, query) * SCORE_SCALE
        local_value_acc[...] += dot(local_weight_low, grad)
        put(tile, row, out_t.T, grad_query_t.astype(BF16).T, top, inverse, row_dot)
        return carry

    lax.fori_loop(0, lax.div(count + TILE_ROWS - 1, TILE_ROWS), body, 0)


def own_kernel(*refs):
    scalars = refs[:5]
    query, grad, keys, values, local_keys, local_values = refs[5:11]
    out, grad_query, local_key, local_value, key_part, value_part = refs[11:]
    own, _, ends = plan(scalars)
    group = query.shape[1] // HEAD_WIDTH
    for ref in (out, grad_query, local_key, local_value, key_part, value_part):
        ref[...] = jnp.zeros(ref.shape, ref.dtype)

    def put(tile, row, out_tile, grad_query_tile, top, inverse, row_dot):
        put_tile(out, row, group, out_tile)
        put_tile(grad_query, row, group, grad_query_tile)

    segment(
        own, 0, ends,
        lambda row: tile_of(query, row, group), lambda row: tile_of(grad, row, group),
        keys[...], values[...], local_keys[...], local_values[...],
        group, put, key_part, value_part, local_key, local_value,
    )


def left_kernel(*refs):
    scalars = refs[:5]
    (rows, keys, values, local_keys, local_values,
     left_out, left_grad_query, key_acc, value_acc, stats) = refs[5:]
    own, total, ends = plan(scalars)
    count = total - own
    step = pl.program_id(0)
    heads = range(keys.shape[1] // HEAD_WIDTH)
    width = rows.shape[2] // len(heads)
    group = width // HEAD_WIDTH
    columns = group * TILE_ROWS
    all_rows = left_out.shape[0]
    for ref in (left_out, left_grad_query, key_acc, value_acc):
        ref[...] = jnp.zeros(ref.shape, ref.dtype)

    @pl.when(step == 0)
    def _():
        stats[...] = jnp.zeros(stats.shape, F32)

    scale2 = SCORE_SCALE * LOG2_E
    parts = chunks(keys.shape[0], KEY_CHUNK)

    def head_columns(head):
        return slice(head * HEAD_WIDTH, (head + 1) * HEAD_WIDTH)

    def body(tile, carry):
        row = pl.multiple_of(tile * TILE_ROWS, TILE_ROWS)
        queries = [tile_of(rows.at[0], row, group, head * width) for head in heads]
        grads = [tile_of(rows.at[1], row, group, head * width) for head in heads]
        within = row + lax.rem(lax.broadcasted_iota(jnp.int32, (columns, 1), 0), TILE_ROWS)
        place = within + own
        start = jnp.zeros((columns, 1), jnp.int32)
        for end in ends:
            start = jnp.where(place >= end, end, start)
        key = lax.broadcasted_iota(jnp.int32, (columns, all_rows), 1)
        allowed = (key >= start) & (key <= place)
        key_parts = [
            [keys[part, head_columns(head)] for part in parts] + [local_keys[:, head_columns(head)]]
            for head in heads
        ]
        value_parts = [
            [values[part, head_columns(head)] for part in parts] + [local_values[:, head_columns(head)]]
            for head in heads
        ]
        weights, tops, inverses = [], [], []
        for head in heads:
            scores = [dot_nt(queries[head], part) * scale2 for part in key_parts[head]]
            scores[-1] = jnp.where(allowed, scores[-1], NEGATIVE)
            top = functools.reduce(
                jnp.maximum, [jnp.max(score, axis=1, keepdims=True) for score in scores]
            )
            exponents = [jnp.exp2(score - top) for score in scores]
            inverse = 1.0 / sum(jnp.sum(part, axis=1, keepdims=True) for part in exponents)
            weights.append([part * inverse for part in exponents])
            tops.append(top)
            inverses.append(inverse)
        low = [[weight.astype(BF16) for weight in weights[head]] for head in heads]
        lane = lax.broadcasted_iota(jnp.int32, (columns, HEAD_WIDTH), 1)
        where = pl.ds(pl.multiple_of(tile * columns, columns), columns)
        for head in heads:
            result = sum(dot(weight, value) for weight, value in zip(low[head], value_parts[head]))
            result = jnp.where(within < count, result, 0.0).astype(BF16)
            row_dot = jnp.sum(
                result.astype(F32) * grads[head].astype(F32), axis=1, keepdims=True
            )
            grad_scores = [
                (weight * (dot_nt(grads[head], value) - row_dot)).astype(BF16)
                for weight, value in zip(weights[head], value_parts[head])
            ]
            grad_rows = sum(dot(score, part) for score, part in zip(grad_scores, key_parts[head]))
            put_tile(left_out, row, group, result, head * width)
            put_tile(left_grad_query, row, group, (grad_rows * SCORE_SCALE).astype(BF16), head * width)
            key_acc[:, head_columns(head)] += dot(grad_scores[-1].T, queries[head]) * SCORE_SCALE
            value_acc[:, head_columns(head)] += dot(low[head][-1].T, grads[head])
            packed = jnp.where(lane == 0, tops[head], jnp.where(lane == 1, inverses[head], row_dot)).T
            stats[pl.ds(pl.multiple_of((step * len(heads) + head) * 8, 8), 8), where] = packed[:8]
        return carry

    lax.fori_loop(0, lax.div(count + TILE_ROWS - 1, TILE_ROWS), body, 0)


def merge_kernel(*refs):
    scalars = refs[:5]
    owns, lefts, outs = refs[5:9], refs[9:13], refs[-4:]
    own, _, _ = plan(scalars)
    rows = outs[0].shape[0]
    target = lax.broadcasted_iota(jnp.int32, (rows, rows), 0)
    source = lax.broadcasted_iota(jnp.int32, (rows, rows), 1)
    place = (target == source + own).astype(BF16)
    for own_rows, left, out in zip(owns[:2], lefts[:2], outs[:2]):
        out[...] = (own_rows[...].astype(F32) + dot(place, left[...])).astype(BF16)
    for own_part, left, out in zip(owns[2:], lefts[2:], outs[2:]):
        out[...] = (own_part[...] + left[...]).astype(BF16)


def arrived_kernel(counts, first, second, stats, keys, values, own_key, own_value, *rest):
    key_out, value_out, key_acc, value_acc = rest[-4:]
    count = counts[1]
    heads = range(keys.shape[1] // HEAD_WIDTH)
    width = first.shape[2] // len(heads)
    group = width // HEAD_WIDTH
    columns = group * TILE_ROWS
    scale2 = SCORE_SCALE * LOG2_E
    key_acc[...] = own_key[...]
    value_acc[...] = own_value[...]
    parts = chunks(keys.shape[0], ARRIVED_CHUNK)
    tiles = lax.div(count + TILE_ROWS - 1, TILE_ROWS)
    full = first.shape[1] // TILE_ROWS

    def steps(rows, first_tile):
        def body(tile, carry):
            row = pl.multiple_of(tile * TILE_ROWS, TILE_ROWS)
            within = first_tile * TILE_ROWS + row + lax.rem(
                lax.broadcasted_iota(jnp.int32, (columns, 1), 0), TILE_ROWS
            )
            where = pl.ds(pl.multiple_of((first_tile + tile) * columns, columns), columns)
            queries, grads = [
                [tile_of(rows.at[index], row, group, head * width) for head in heads]
                for index in range(2)
            ]
            if first_tile:
                queries, grads = [
                    [jnp.where(within < count, tile, 0) for tile in tiles]
                    for tiles in (queries, grads)
                ]
            for part in parts:
                for head in heads:
                    here = slice(head * HEAD_WIDTH, (head + 1) * HEAD_WIDTH)
                    stat = stats[pl.ds(head * 8, 8), where]
                    weight = jnp.exp2(
                        dot_nt(keys[part, here], queries[head]) * scale2 - stat[0:1]
                    ) * stat[1:2]
                    grad_scores = (
                        weight * (dot_nt(values[part, here], grads[head]) - stat[2:3])
                    ).astype(BF16)
                    key_acc[part, here] += dot(grad_scores, queries[head])
                    value_acc[part, here] += dot(weight.astype(BF16), grads[head])
            return carry

        return body

    lax.fori_loop(0, jnp.minimum(tiles, full), steps(first, 0), 0)
    lax.fori_loop(0, jnp.maximum(tiles - full, 0), steps(second, full), 0)
    key_out[0] = (key_acc[...] * SCORE_SCALE).astype(BF16)
    value_out[0] = value_acc[...].astype(BF16)


def after(values, others):
    count = len(values)
    return pl.pallas_call(
        lambda *refs: None,
        in_specs=[pl.BlockSpec(memory_space=pl.ANY)] * (count + len(others)),
        out_specs=[pl.BlockSpec(memory_space=pl.ANY)] * count,
        out_shape=[jax.ShapeDtypeStruct(value.shape, value.dtype) for value in values],
        input_output_aliases={k: k for k in range(count)},
        name="after",
    )(*values, *others)


def send_late(late, send_count, receive_count, device):
    devices = lax.axis_size("dp")
    half = late.shape[1]
    if devices % 2:
        return shifted(late, "dp", -1)
    sizes = [size for size in (0, 8, 16, 32) if size < half] + [half]
    even = lax.rem(device, 2) == 0

    def branch(pairs, receives, size):
        def send(value, received):
            if size == 0:
                return received
            got = lax.ppermute(value[:, :size], "dp", pairs)
            got = jnp.pad(got, ((0, 0), (0, half - size), (0, 0)))
            return jnp.where(receives, got, received)

        return send

    received = late
    for parity in range(2):
        pairs = [(b, (b - 1) % devices) for b in range(parity, devices, 2)]
        sends = even == (parity == 0)
        count = jnp.where(sends, send_count, receive_count)
        choice = sum((count > half + size).astype(jnp.int32) for size in sizes[:-1])
        branches = [branch(pairs, jnp.logical_not(sends), size) for size in sizes]
        received = lax.switch(choice, branches, late, received)
    return received


def per_device(
    queries, response_key_rows, response_value_rows, shared_prompt_keys, shared_prompt_values,
    grad_out, lengths, packing, prompt_of, prompt_owner,
):
    rows = queries.shape[0]
    kv_heads = response_key_rows.shape[1] // HEAD_WIDTH
    width = queries.shape[1] // kv_heads
    prompt = shared_prompt_keys.shape[1]
    device = lax.axis_index("dp").astype(jnp.int32).reshape(1)
    scalars = (device, packing, lengths, prompt_of, prompt_owner)
    smem = [pl.BlockSpec(memory_space=pltpu.SMEM)] * 5
    params = pltpu.CompilerParams(vmem_limit_bytes=VMEM_LIMIT)
    cost = pl.CostEstimate(flops=1, bytes_accessed=1, transcendentals=0)
    shape = jax.ShapeDtypeStruct
    wide = pl.BlockSpec((rows, width), lambda h: (0, h))
    narrow = pl.BlockSpec((rows, HEAD_WIDTH), lambda h: (0, h))
    context = pl.BlockSpec((prompt, HEAD_WIDTH), lambda h: (0, h))
    pair = pl.BlockSpec((2, rows, width), lambda h: (0, 0, h))
    own_keys = shared_prompt_keys[0]
    own_values = shared_prompt_values[0]
    stat_columns = rows * width // HEAD_WIDTH

    left_keys = shifted(own_keys, "dp", 1)
    left_values = shifted(own_values, "dp", 1)

    half = rows // 2
    moved, early, late, counts = pl.pallas_call(
        gather_kernel,
        grid=(1,),
        in_specs=smem + [pl.BlockSpec(queries.shape, lambda i: (0, 0))] * 2,
        out_specs=[
            pl.BlockSpec((2, rows, queries.shape[1]), lambda i: (0, 0, 0)),
            pl.BlockSpec((2, half, queries.shape[1]), lambda i: (0, 0, 0)),
            pl.BlockSpec((2, half, queries.shape[1]), lambda i: (0, 0, 0)),
            pl.BlockSpec(memory_space=pltpu.SMEM),
        ],
        out_shape=[
            shape((2, rows, queries.shape[1]), BF16),
            shape((2, half, queries.shape[1]), BF16), shape((2, half, queries.shape[1]), BF16),
            shape((2,), jnp.int32),
        ],
        compiler_params=params,
        cost_estimate=cost,
        name="gather_rows",
    )(*scalars, queries, grad_out)

    own_out, own_grad_query, own_local_key, own_local_value, own_key, own_value = pl.pallas_call(
        own_kernel,
        grid=(kv_heads,),
        in_specs=smem + [wide, wide, context, context, narrow, narrow],
        out_specs=[wide, wide, narrow, narrow, context, context],
        out_shape=[
            shape(queries.shape, BF16), shape(queries.shape, BF16),
            shape(response_key_rows.shape, F32), shape(response_key_rows.shape, F32),
            shape(own_keys.shape, F32), shape(own_keys.shape, F32),
        ],
        compiler_params=params,
        cost_estimate=cost,
        name="own_rows",
    )(*scalars, queries, grad_out, own_keys, own_values, response_key_rows, response_value_rows)

    both = kv_heads // 2
    context_both = pl.BlockSpec((prompt, both * HEAD_WIDTH), lambda h: (0, h))

    wide_both = pl.BlockSpec((rows, both * width), lambda h: (0, h))
    narrow_both = pl.BlockSpec((rows, both * HEAD_WIDTH), lambda h: (0, h))
    pair_both = pl.BlockSpec((2, rows, both * width), lambda h: (0, 0, h))
    early, left_values = after((early, left_values), (left_keys, own_out))
    left_out, left_grad_query, left_local_key, left_local_value, stats = pl.pallas_call(
        left_kernel,
        grid=(2,),
        in_specs=smem + [pair_both, context_both, context_both, narrow_both, narrow_both],
        out_specs=[
            wide_both, wide_both, narrow_both, narrow_both,
            pl.BlockSpec((8 * kv_heads, stat_columns), lambda h: (0, 0)),
        ],
        out_shape=[
            shape(queries.shape, BF16), shape(queries.shape, BF16),
            shape(response_key_rows.shape, F32), shape(response_key_rows.shape, F32),
            shape((8 * kv_heads, stat_columns), F32),
        ],
        compiler_params=params,
        cost_estimate=cost,
        name="left_rows",
    )(*scalars, moved, left_keys, left_values, response_key_rows, response_value_rows)

    out, grad_query, local_key, local_value = pl.pallas_call(
        merge_kernel,
        grid=(kv_heads,),
        in_specs=smem + [wide, wide, narrow, narrow] * 2,
        out_specs=[wide, wide, narrow, narrow],
        out_shape=[
            shape(queries.shape, BF16), shape(queries.shape, BF16),
            shape(response_key_rows.shape, BF16), shape(response_key_rows.shape, BF16),
        ],
        compiler_params=params,
        cost_estimate=cost,
        name="merge_rows",
    )(*scalars, own_out, own_grad_query, own_local_key, own_local_value,
      left_out, left_grad_query, left_local_key, left_local_value)

    (late,) = after((late,), (out,))
    arrived_second = send_late(late, counts[0], counts[1], device[0])
    half_rows = pl.BlockSpec((2, half, both * width), lambda h: (0, 0, h))
    whole = pl.BlockSpec((1, prompt, both * HEAD_WIDTH), lambda h: (0, 0, h))
    prompt_key, prompt_value = pl.pallas_call(
        arrived_kernel,
        grid=(2,),
        in_specs=[
            pl.BlockSpec(memory_space=pltpu.SMEM), half_rows, half_rows,
            pl.BlockSpec((8 * both, stat_columns), lambda h: (h, 0)),
        ] + [context_both] * 4,
        out_specs=[whole, whole],
        out_shape=[shape((1,) + own_keys.shape, BF16)] * 2,
        scratch_shapes=[pltpu.VMEM((prompt, both * HEAD_WIDTH), F32)] * 2,
        compiler_params=params,
        cost_estimate=cost,
        name="arrived_rows",
    )(counts, shifted(early, "dp", -1), arrived_second, shifted(stats, "dp", -1),
      own_keys, own_values, own_key, own_value)
    return out, grad_query, local_key, local_value, prompt_key, prompt_value


def solution(mesh):
    rows = P(("groups", "dp"), "tensor")
    prompts = P(("groups", "dp"), None, "tensor")
    in_specs = (
        rows, rows, rows, prompts, prompts, rows,
        P("groups"), P(("groups", "dp"), None), P("groups"), P("groups"),
    )
    out_specs = (rows, rows, rows, rows, prompts, prompts)
    return jax.shard_map(
        per_device, mesh=mesh, in_specs=in_specs, out_specs=out_specs, check_vma=False
    )
```

```python
import functools

import jax
import jax.numpy as jnp
from jax import lax
from jax.experimental import pallas as pl
from jax.experimental.pallas import tpu as pltpu
from jax.sharding import PartitionSpec as P

HEAD_WIDTH = 128
TILE_ROWS = 32
SCORE_SCALE = HEAD_WIDTH ** -0.5
LOG2_E = 1.4426950408889634
NEGATIVE = -1e30
F32 = jnp.float32
BF16 = jnp.bfloat16
VMEM_LIMIT = 64 * 1024 * 1024
KEY_CHUNK = 256
ARRIVED_CHUNK = 768


def shifted(value, axis, steps):
    count = lax.axis_size(axis)
    pairs = [(source, (source + steps) % count) for source in range(count)]
    return lax.ppermute(value, axis, pairs)


def dot(left, right):
    return lax.dot_general(
        left, right, (((1,), (0,)), ((), ())), preferred_element_type=F32
    )


def dot_nt(left, right):
    return lax.dot_general(
        left, right, (((1,), (1,)), ((), ())), preferred_element_type=F32
    )


def chunks(length, size):
    return [slice(start, min(start + size, length)) for start in range(0, length, size)]


def plan(scalars):
    device, packing, lengths, prompt_of, prompt_owner = scalars
    own = jnp.int32(0)
    total = jnp.int32(0)
    ends = []
    for slot in range(packing.shape[1]):
        entry = packing[0, slot]
        used = entry >= 0
        index = jnp.maximum(entry, 0)
        length = jnp.where(used, lengths[index], 0)
        holder = prompt_owner[prompt_of[index]]
        own = own + jnp.where(holder == device[0], length, 0)
        total = total + length
        ends.append(total)
    return own, total, ends


def tile_of(ref, row, group, first=0):
    columns = [slice(first + g * HEAD_WIDTH, first + (g + 1) * HEAD_WIDTH) for g in range(group)]
    return jnp.concatenate([ref[pl.ds(row, TILE_ROWS), part] for part in columns], axis=0)


def put_tile(ref, row, group, value, first=0):
    for g in range(group):
        columns = slice(first + g * HEAD_WIDTH, first + (g + 1) * HEAD_WIDTH)
        ref[pl.ds(row, TILE_ROWS), columns] = value[g * TILE_ROWS : (g + 1) * TILE_ROWS]


def local_mask(first_row, ends, keys, columns):
    column = lax.broadcasted_iota(jnp.int32, (1, columns), 1)
    row = first_row + lax.rem(column, TILE_ROWS)
    start = jnp.zeros((1, columns), jnp.int32)
    for end in ends:
        start = jnp.where(row >= end, end, start)
    key = lax.broadcasted_iota(jnp.int32, (keys, columns), 0)
    return (key >= start) & (key <= row)


def gather_kernel(*refs):
    scalars = refs[:5]
    query, grad, moved_out, early_out, late_out, counts_out = refs[5:]
    own, total, _ = plan(scalars)
    device, _, lengths, prompt_of, prompt_owner = scalars

    def add(response, sum_of_mine):
        mine = prompt_owner[prompt_of[response]] == device[0]
        return sum_of_mine + jnp.where(mine, lengths[response], 0)

    counts_out[0] = total - own
    counts_out[1] = lax.fori_loop(0, lengths.shape[0], add, jnp.int32(0)) - own
    rows = query.shape[0]
    half = rows // 2
    target = lax.broadcasted_iota(jnp.int32, (rows, rows), 0)
    source = lax.broadcasted_iota(jnp.int32, (rows, rows), 1)
    pick = ((source == target + own) & (source < total)).astype(BF16)
    for index, ref in enumerate((query, grad)):
        picked = dot(pick, ref[...]).astype(BF16)
        moved_out[index] = picked
        early_out[index] = picked[:half]
        late_out[index] = picked[half:]


def segment(
    count, offset, ends, query_tile, grad_tile, keys, values, local_keys, local_values,
    group, put, key_acc, value_acc, local_key_acc, local_value_acc,
):
    columns = group * TILE_ROWS
    keys_t = keys.T
    values_t = values.T
    local_keys_t = local_keys.T
    local_values_t = local_values.T
    scale2 = SCORE_SCALE * LOG2_E

    def body(tile, carry):
        row = pl.multiple_of(tile * TILE_ROWS, TILE_ROWS)
        within = row + lax.rem(lax.broadcasted_iota(jnp.int32, (columns, 1), 0), TILE_ROWS)
        query = jnp.where(within < count, query_tile(row), 0)
        grad = jnp.where(within < count, grad_tile(row), 0)
        query_t = query.T
        grad_t = grad.T
        within_t = row + lax.rem(lax.broadcasted_iota(jnp.int32, (1, columns), 1), TILE_ROWS)
        allowed = local_mask(row + offset, ends, local_keys.shape[0], columns)
        scores = dot(keys, query_t) * scale2
        local_scores = jnp.where(allowed, dot(local_keys, query_t) * scale2, NEGATIVE)
        top = jnp.maximum(
            jnp.max(scores, axis=0, keepdims=True), jnp.max(local_scores, axis=0, keepdims=True)
        )
        weight = jnp.exp2(scores - top)
        local_weight = jnp.exp2(local_scores - top)
        inverse = 1.0 / (
            jnp.sum(weight, axis=0, keepdims=True) + jnp.sum(local_weight, axis=0, keepdims=True)
        )
        weight = weight * inverse
        local_weight = local_weight * inverse
        weight_low = weight.astype(BF16)
        local_weight_low = local_weight.astype(BF16)
        out_t = dot(values_t, weight_low) + dot(local_values_t, local_weight_low)
        out_t = jnp.where(within_t < count, out_t, 0.0).astype(BF16)
        row_dot = jnp.sum(out_t.astype(F32) * grad_t.astype(F32), axis=0, keepdims=True)
        grad_scores = (weight * (dot(values, grad_t) - row_dot)).astype(BF16)
        local_grad_scores = (local_weight * (dot(local_values, grad_t) - row_dot)).astype(BF16)
        grad_query_t = (
            dot(keys_t, grad_scores) + dot(local_keys_t, local_grad_scores)
        ) * SCORE_SCALE
        if key_acc is not None:
            key_acc[...] += dot(grad_scores, query)
            value_acc[...] += dot(weight_low, grad)
        local_key_acc[...] += dot(local_grad_scores, query) * SCORE_SCALE
        local_value_acc[...] += dot(local_weight_low, grad)
        put(tile, row, out_t.T, grad_query_t.astype(BF16).T, top, inverse, row_dot)
        return carry

    lax.fori_loop(0, lax.div(count + TILE_ROWS - 1, TILE_ROWS), body, 0)


def own_kernel(*refs):
    scalars = refs[:5]
    query, grad, keys, values, local_keys, local_values = refs[5:11]
    out, grad_query, local_key, local_value, key_part, value_part = refs[11:]
    own, _, ends = plan(scalars)
    group = query.shape[1] // HEAD_WIDTH
    for ref in (out, grad_query, local_key, local_value, key_part, value_part):
        ref[...] = jnp.zeros(ref.shape, ref.dtype)

    def put(tile, row, out_tile, grad_query_tile, top, inverse, row_dot):
        put_tile(out, row, group, out_tile)
        put_tile(grad_query, row, group, grad_query_tile)

    segment(
        own, 0, ends,
        lambda row: tile_of(query, row, group), lambda row: tile_of(grad, row, group),
        keys[...], values[...], local_keys[...], local_values[...],
        group, put, key_part, value_part, local_key, local_value,
    )


def left_kernel(*refs):
    scalars = refs[:5]
    (rows, keys, values, local_keys, local_values,
     left_out, left_grad_query, key_acc, value_acc, stats) = refs[5:]
    own, total, ends = plan(scalars)
    count = total - own
    heads = range(keys.shape[1] // HEAD_WIDTH)
    width = rows.shape[2] // len(heads)
    group = width // HEAD_WIDTH
    columns = group * TILE_ROWS
    all_rows = left_out.shape[0]
    for ref in (left_out, left_grad_query, key_acc, value_acc, stats):
        ref[...] = jnp.zeros(ref.shape, ref.dtype)

    scale2 = SCORE_SCALE * LOG2_E
    parts = chunks(keys.shape[0], KEY_CHUNK)

    def head_columns(head):
        return slice(head * HEAD_WIDTH, (head + 1) * HEAD_WIDTH)

    def body(tile, carry):
        row = pl.multiple_of(tile * TILE_ROWS, TILE_ROWS)
        queries = [tile_of(rows.at[0], row, group, head * width) for head in heads]
        grads = [tile_of(rows.at[1], row, group, head * width) for head in heads]
        within = row + lax.rem(lax.broadcasted_iota(jnp.int32, (columns, 1), 0), TILE_ROWS)
        place = within + own
        start = jnp.zeros((columns, 1), jnp.int32)
        for end in ends:
            start = jnp.where(place >= end, end, start)
        key = lax.broadcasted_iota(jnp.int32, (columns, all_rows), 1)
        allowed = (key >= start) & (key <= place)
        key_parts = [
            [keys[part, head_columns(head)] for part in parts] + [local_keys[:, head_columns(head)]]
            for head in heads
        ]
        value_parts = [
            [values[part, head_columns(head)] for part in parts] + [local_values[:, head_columns(head)]]
            for head in heads
        ]
        weights, tops, inverses = [], [], []
        for head in heads:
            scores = [dot_nt(queries[head], part) * scale2 for part in key_parts[head]]
            scores[-1] = jnp.where(allowed, scores[-1], NEGATIVE)
            top = functools.reduce(
                jnp.maximum, [jnp.max(score, axis=1, keepdims=True) for score in scores]
            )
            exponents = [jnp.exp2(score - top) for score in scores]
            inverse = 1.0 / sum(jnp.sum(part, axis=1, keepdims=True) for part in exponents)
            weights.append([part * inverse for part in exponents])
            tops.append(top)
            inverses.append(inverse)
        low = [[weight.astype(BF16) for weight in weights[head]] for head in heads]
        lane = lax.broadcasted_iota(jnp.int32, (columns, HEAD_WIDTH), 1)
        where = pl.ds(pl.multiple_of(tile * columns, columns), columns)
        for head in heads:
            result = sum(dot(weight, value) for weight, value in zip(low[head], value_parts[head]))
            result = jnp.where(within < count, result, 0.0).astype(BF16)
            row_dot = jnp.sum(
                result.astype(F32) * grads[head].astype(F32), axis=1, keepdims=True
            )
            grad_scores = [
                (weight * (dot_nt(grads[head], value) - row_dot)).astype(BF16)
                for weight, value in zip(weights[head], value_parts[head])
            ]
            grad_rows = sum(dot(score, part) for score, part in zip(grad_scores, key_parts[head]))
            put_tile(left_out, row, group, result, head * width)
            put_tile(left_grad_query, row, group, (grad_rows * SCORE_SCALE).astype(BF16), head * width)
            key_acc[:, head_columns(head)] += dot(grad_scores[-1].T, queries[head]) * SCORE_SCALE
            value_acc[:, head_columns(head)] += dot(low[head][-1].T, grads[head])
            packed = jnp.where(lane == 0, tops[head], jnp.where(lane == 1, inverses[head], row_dot)).T
            stats[head * 4 : (head + 1) * 4, where] = packed[:4]
        return carry

    lax.fori_loop(0, lax.div(count + TILE_ROWS - 1, TILE_ROWS), body, 0)


def merge_kernel(*refs):
    scalars = refs[:5]
    owns, lefts, outs = refs[5:9], refs[9:13], refs[-4:]
    own, _, _ = plan(scalars)
    rows = outs[0].shape[0]
    target = lax.broadcasted_iota(jnp.int32, (rows, rows), 0)
    source = lax.broadcasted_iota(jnp.int32, (rows, rows), 1)
    place = (target == source + own).astype(BF16)
    for own_rows, left, out in zip(owns[:2], lefts[:2], outs[:2]):
        out[...] = (own_rows[...].astype(F32) + dot(place, left[...])).astype(BF16)
    for own_part, left, out in zip(owns[2:], lefts[2:], outs[2:]):
        out[...] = (own_part[...] + left[...]).astype(BF16)


def arrived_kernel(counts, first, second, stats, keys, values, own_key, own_value, *rest):
    key_out, value_out, key_acc, value_acc = rest[-4:]
    count = counts[1]
    heads = range(keys.shape[1] // HEAD_WIDTH)
    width = first.shape[2] // len(heads)
    group = width // HEAD_WIDTH
    columns = group * TILE_ROWS
    scale2 = SCORE_SCALE * LOG2_E
    key_acc[...] = own_key[...]
    value_acc[...] = own_value[...]
    parts = chunks(keys.shape[0], ARRIVED_CHUNK)
    tiles = lax.div(count + TILE_ROWS - 1, TILE_ROWS)
    full = first.shape[1] // TILE_ROWS

    def steps(rows, first_tile):
        def body(tile, carry):
            row = pl.multiple_of(tile * TILE_ROWS, TILE_ROWS)
            within = first_tile * TILE_ROWS + row + lax.rem(
                lax.broadcasted_iota(jnp.int32, (columns, 1), 0), TILE_ROWS
            )
            where = pl.ds(pl.multiple_of((first_tile + tile) * columns, columns), columns)
            queries, grads = [
                [tile_of(rows.at[index], row, group, head * width) for head in heads]
                for index in range(2)
            ]
            if first_tile:
                queries, grads = [
                    [jnp.where(within < count, tile, 0) for tile in tiles]
                    for tiles in (queries, grads)
                ]
            for part in parts:
                for head in heads:
                    here = slice(head * HEAD_WIDTH, (head + 1) * HEAD_WIDTH)
                    stat = stats[head * 4 : (head + 1) * 4, where]
                    weight = jnp.exp2(
                        dot_nt(keys[part, here], queries[head]) * scale2 - stat[0:1]
                    ) * stat[1:2]
                    grad_scores = (
                        weight * (dot_nt(values[part, here], grads[head]) - stat[2:3])
                    ).astype(BF16)
                    key_acc[part, here] += dot(grad_scores, queries[head])
                    value_acc[part, here] += dot(weight.astype(BF16), grads[head])
            return carry

        return body

    lax.fori_loop(0, jnp.minimum(tiles, full), steps(first, 0), 0)
    lax.fori_loop(0, jnp.maximum(tiles - full, 0), steps(second, full), 0)
    key_out[0] = (key_acc[...] * SCORE_SCALE).astype(BF16)
    value_out[0] = value_acc[...].astype(BF16)


def after(values, others):
    count = len(values)
    return pl.pallas_call(
        lambda *refs: None,
        in_specs=[pl.BlockSpec(memory_space=pl.ANY)] * (count + len(others)),
        out_specs=[pl.BlockSpec(memory_space=pl.ANY)] * count,
        out_shape=[jax.ShapeDtypeStruct(value.shape, value.dtype) for value in values],
        input_output_aliases={k: k for k in range(count)},
        name="after",
    )(*values, *others)


def send_late(late, send_count, receive_count, device):
    devices = lax.axis_size("dp")
    half = late.shape[1]
    if devices % 2:
        return shifted(late, "dp", -1)
    sizes = [size for size in (0, 8, 16, 32) if size < half] + [half]
    even = lax.rem(device, 2) == 0

    def branch(pairs, receives, size):
        def send(value, received):
            if size == 0:
                return received
            got = lax.ppermute(value[:, :size], "dp", pairs)
            got = jnp.pad(got, ((0, 0), (0, half - size), (0, 0)))
            return jnp.where(receives, got, received)

        return send

    received = late
    for parity in range(2):
        pairs = [(b, (b - 1) % devices) for b in range(parity, devices, 2)]
        sends = even == (parity == 0)
        count = jnp.where(sends, send_count, receive_count)
        choice = sum((count > half + size).astype(jnp.int32) for size in sizes[:-1])
        branches = [branch(pairs, jnp.logical_not(sends), size) for size in sizes]
        received = lax.switch(choice, branches, late, received)
    return received


def per_device(
    queries, response_key_rows, response_value_rows, shared_prompt_keys, shared_prompt_values,
    grad_out, lengths, packing, prompt_of, prompt_owner,
):
    rows = queries.shape[0]
    kv_heads = response_key_rows.shape[1] // HEAD_WIDTH
    width = queries.shape[1] // kv_heads
    prompt = shared_prompt_keys.shape[1]
    device = lax.axis_index("dp").astype(jnp.int32).reshape(1)
    scalars = (device, packing, lengths, prompt_of, prompt_owner)
    smem = [pl.BlockSpec(memory_space=pltpu.SMEM)] * 5
    params = pltpu.CompilerParams(vmem_limit_bytes=VMEM_LIMIT)
    cost = pl.CostEstimate(flops=1, bytes_accessed=1, transcendentals=0)
    shape = jax.ShapeDtypeStruct
    wide = pl.BlockSpec((rows, width), lambda h: (0, h))
    narrow = pl.BlockSpec((rows, HEAD_WIDTH), lambda h: (0, h))
    context = pl.BlockSpec((prompt, HEAD_WIDTH), lambda h: (0, h))
    pair = pl.BlockSpec((2, rows, width), lambda h: (0, 0, h))
    own_keys = shared_prompt_keys[0]
    own_values = shared_prompt_values[0]
    stat_columns = rows * width // HEAD_WIDTH

    left_keys = shifted(own_keys, "dp", 1)
    left_values = shifted(own_values, "dp", 1)

    half = rows // 2
    moved, early, late, counts = pl.pallas_call(
        gather_kernel,
        grid=(1,),
        in_specs=smem + [pl.BlockSpec(queries.shape, lambda i: (0, 0))] * 2,
        out_specs=[
            pl.BlockSpec((2, rows, queries.shape[1]), lambda i: (0, 0, 0)),
            pl.BlockSpec((2, half, queries.shape[1]), lambda i: (0, 0, 0)),
            pl.BlockSpec((2, half, queries.shape[1]), lambda i: (0, 0, 0)),
            pl.BlockSpec(memory_space=pltpu.SMEM),
        ],
        out_shape=[
            shape((2, rows, queries.shape[1]), BF16),
            shape((2, half, queries.shape[1]), BF16), shape((2, half, queries.shape[1]), BF16),
            shape((2,), jnp.int32),
        ],
        compiler_params=params,
        cost_estimate=cost,
        name="gather_rows",
    )(*scalars, queries, grad_out)

    own_out, own_grad_query, own_local_key, own_local_value, own_key, own_value = pl.pallas_call(
        own_kernel,
        grid=(kv_heads,),
        in_specs=smem + [wide, wide, context, context, narrow, narrow],
        out_specs=[wide, wide, narrow, narrow, context, context],
        out_shape=[
            shape(queries.shape, BF16), shape(queries.shape, BF16),
            shape(response_key_rows.shape, F32), shape(response_key_rows.shape, F32),
            shape(own_keys.shape, F32), shape(own_keys.shape, F32),
        ],
        compiler_params=params,
        cost_estimate=cost,
        name="own_rows",
    )(*scalars, queries, grad_out, own_keys, own_values, response_key_rows, response_value_rows)

    both = kv_heads // 2
    context_both = pl.BlockSpec((prompt, both * HEAD_WIDTH), lambda h: (0, h))

    wide_both = pl.BlockSpec((rows, both * width), lambda h: (0, h))
    narrow_both = pl.BlockSpec((rows, both * HEAD_WIDTH), lambda h: (0, h))
    pair_both = pl.BlockSpec((2, rows, both * width), lambda h: (0, 0, h))
    early, left_values = after((early, left_values), (left_keys, own_out))
    left_out, left_grad_query, left_local_key, left_local_value, stats = pl.pallas_call(
        left_kernel,
        grid=(2,),
        in_specs=smem + [pair_both, context_both, context_both, narrow_both, narrow_both],
        out_specs=[
            wide_both, wide_both, narrow_both, narrow_both,
            pl.BlockSpec((4 * both, stat_columns), lambda h: (h, 0)),
        ],
        out_shape=[
            shape(queries.shape, BF16), shape(queries.shape, BF16),
            shape(response_key_rows.shape, F32), shape(response_key_rows.shape, F32),
            shape((4 * kv_heads, stat_columns), F32),
        ],
        compiler_params=params,
        cost_estimate=cost,
        name="left_rows",
    )(*scalars, moved, left_keys, left_values, response_key_rows, response_value_rows)

    out, grad_query, local_key, local_value = pl.pallas_call(
        merge_kernel,
        grid=(kv_heads,),
        in_specs=smem + [wide, wide, narrow, narrow] * 2,
        out_specs=[wide, wide, narrow, narrow],
        out_shape=[
            shape(queries.shape, BF16), shape(queries.shape, BF16),
            shape(response_key_rows.shape, BF16), shape(response_key_rows.shape, BF16),
        ],
        compiler_params=params,
        cost_estimate=cost,
        name="merge_rows",
    )(*scalars, own_out, own_grad_query, own_local_key, own_local_value,
      left_out, left_grad_query, left_local_key, left_local_value)

    (late,) = after((late,), (out,))
    arrived_second = send_late(late, counts[0], counts[1], device[0])
    half_rows = pl.BlockSpec((2, half, both * width), lambda h: (0, 0, h))
    whole = pl.BlockSpec((1, prompt, both * HEAD_WIDTH), lambda h: (0, 0, h))
    prompt_key, prompt_value = pl.pallas_call(
        arrived_kernel,
        grid=(2,),
        in_specs=[
            pl.BlockSpec(memory_space=pltpu.SMEM), half_rows, half_rows,
            pl.BlockSpec((4 * both, stat_columns), lambda h: (h, 0)),
        ] + [context_both] * 4,
        out_specs=[whole, whole],
        out_shape=[shape((1,) + own_keys.shape, BF16)] * 2,
        scratch_shapes=[pltpu.VMEM((prompt, both * HEAD_WIDTH), F32)] * 2,
        compiler_params=params,
        cost_estimate=cost,
        name="arrived_rows",
    )(counts, shifted(early, "dp", -1), arrived_second, shifted(stats, "dp", -1),
      own_keys, own_values, own_key, own_value)
    return out, grad_query, local_key, local_value, prompt_key, prompt_value


def solution(mesh):
    rows = P(("groups", "dp"), "tensor")
    prompts = P(("groups", "dp"), None, "tensor")
    in_specs = (
        rows, rows, rows, prompts, prompts, rows,
        P("groups"), P(("groups", "dp"), None), P("groups"), P("groups"),
    )
    out_specs = (rows, rows, rows, rows, prompts, prompts)
    return jax.shard_map(
        per_device, mesh=mesh, in_specs=in_specs, out_specs=out_specs, check_vma=False
    )
```

```python
import functools

import jax
import jax.numpy as jnp
from jax import lax
from jax.experimental import pallas as pl
from jax.experimental.pallas import tpu as pltpu
from jax.sharding import PartitionSpec as P

HEAD_WIDTH = 128
TILE_ROWS = 32
SCORE_SCALE = HEAD_WIDTH ** -0.5
LOG2_E = 1.4426950408889634
NEGATIVE = -1e30
F32 = jnp.float32
BF16 = jnp.bfloat16
VMEM_LIMIT = 64 * 1024 * 1024
KEY_CHUNK = 256
ARRIVED_CHUNK = 768


def shifted(value, axis, steps):
    count = lax.axis_size(axis)
    pairs = [(source, (source + steps) % count) for source in range(count)]
    return lax.ppermute(value, axis, pairs)


def dot(left, right):
    return lax.dot_general(
        left, right, (((1,), (0,)), ((), ())), preferred_element_type=F32
    )


def dot_nt(left, right):
    return lax.dot_general(
        left, right, (((1,), (1,)), ((), ())), preferred_element_type=F32
    )


def chunks(length, size):
    return [slice(start, min(start + size, length)) for start in range(0, length, size)]


def plan(scalars):
    device, packing, lengths, prompt_of, prompt_owner = scalars
    own = jnp.int32(0)
    total = jnp.int32(0)
    ends = []
    for slot in range(packing.shape[1]):
        entry = packing[0, slot]
        used = entry >= 0
        index = jnp.maximum(entry, 0)
        length = jnp.where(used, lengths[index], 0)
        holder = prompt_owner[prompt_of[index]]
        own = own + jnp.where(holder == device[0], length, 0)
        total = total + length
        ends.append(total)
    return own, total, ends


def tile_of(ref, row, group, first=0):
    columns = [slice(first + g * HEAD_WIDTH, first + (g + 1) * HEAD_WIDTH) for g in range(group)]
    return jnp.concatenate([ref[pl.ds(row, TILE_ROWS), part] for part in columns], axis=0)


def put_tile(ref, row, group, value, first=0):
    for g in range(group):
        columns = slice(first + g * HEAD_WIDTH, first + (g + 1) * HEAD_WIDTH)
        ref[pl.ds(row, TILE_ROWS), columns] = value[g * TILE_ROWS : (g + 1) * TILE_ROWS]


def local_mask(first_row, ends, keys, columns):
    column = lax.broadcasted_iota(jnp.int32, (1, columns), 1)
    row = first_row + lax.rem(column, TILE_ROWS)
    start = jnp.zeros((1, columns), jnp.int32)
    for end in ends:
        start = jnp.where(row >= end, end, start)
    key = lax.broadcasted_iota(jnp.int32, (keys, columns), 0)
    return (key >= start) & (key <= row)


def gather_kernel(*refs):
    scalars = refs[:5]
    query, grad, moved_out, early_out, late_out, counts_out = refs[5:]
    own, total, _ = plan(scalars)
    device, _, lengths, prompt_of, prompt_owner = scalars

    def add(response, sum_of_mine):
        mine = prompt_owner[prompt_of[response]] == device[0]
        return sum_of_mine + jnp.where(mine, lengths[response], 0)

    counts_out[0] = total - own
    counts_out[1] = lax.fori_loop(0, lengths.shape[0], add, jnp.int32(0)) - own
    rows = query.shape[0]
    half = rows // 2
    target = lax.broadcasted_iota(jnp.int32, (rows, rows), 0)
    source = lax.broadcasted_iota(jnp.int32, (rows, rows), 1)
    pick = ((source == target + own) & (source < total)).astype(BF16)
    for index, ref in enumerate((query, grad)):
        picked = dot(pick, ref[...]).astype(BF16)
        moved_out[index] = picked
        early_out[index] = picked[:half]
        late_out[index] = picked[half:]


def segment(
    count, offset, ends, query_tile, grad_tile, keys, values, local_keys, local_values,
    group, put, key_acc, value_acc, local_key_acc, local_value_acc,
):
    columns = group * TILE_ROWS
    keys_t = keys.T
    values_t = values.T
    local_keys_t = local_keys.T
    local_values_t = local_values.T
    scale2 = SCORE_SCALE * LOG2_E

    def body(tile, carry):
        row = pl.multiple_of(tile * TILE_ROWS, TILE_ROWS)
        within = row + lax.rem(lax.broadcasted_iota(jnp.int32, (columns, 1), 0), TILE_ROWS)
        query = jnp.where(within < count, query_tile(row), 0)
        grad = jnp.where(within < count, grad_tile(row), 0)
        query_t = query.T
        grad_t = grad.T
        within_t = row + lax.rem(lax.broadcasted_iota(jnp.int32, (1, columns), 1), TILE_ROWS)
        allowed = local_mask(row + offset, ends, local_keys.shape[0], columns)
        scores = dot(keys, query_t) * scale2
        local_scores = jnp.where(allowed, dot(local_keys, query_t) * scale2, NEGATIVE)
        top = jnp.maximum(
            jnp.max(scores, axis=0, keepdims=True), jnp.max(local_scores, axis=0, keepdims=True)
        )
        weight = jnp.exp2(scores - top)
        local_weight = jnp.exp2(local_scores - top)
        inverse = 1.0 / (
            jnp.sum(weight, axis=0, keepdims=True) + jnp.sum(local_weight, axis=0, keepdims=True)
        )
        weight = weight * inverse
        local_weight = local_weight * inverse
        weight_low = weight.astype(BF16)
        local_weight_low = local_weight.astype(BF16)
        out_t = dot(values_t, weight_low) + dot(local_values_t, local_weight_low)
        out_t = jnp.where(within_t < count, out_t, 0.0).astype(BF16)
        row_dot = jnp.sum(out_t.astype(F32) * grad_t.astype(F32), axis=0, keepdims=True)
        grad_scores = (weight * (dot(values, grad_t) - row_dot)).astype(BF16)
        local_grad_scores = (local_weight * (dot(local_values, grad_t) - row_dot)).astype(BF16)
        grad_query_t = (
            dot(keys_t, grad_scores) + dot(local_keys_t, local_grad_scores)
        ) * SCORE_SCALE
        if key_acc is not None:
            key_acc[...] += dot(grad_scores, query)
            value_acc[...] += dot(weight_low, grad)
        local_key_acc[...] += dot(local_grad_scores, query) * SCORE_SCALE
        local_value_acc[...] += dot(local_weight_low, grad)
        put(tile, row, out_t.T, grad_query_t.astype(BF16).T, top, inverse, row_dot)
        return carry

    lax.fori_loop(0, lax.div(count + TILE_ROWS - 1, TILE_ROWS), body, 0)


def own_kernel(*refs):
    scalars = refs[:5]
    query, grad, keys, values, local_keys, local_values = refs[5:11]
    out, grad_query, local_key, local_value, key_part, value_part = refs[11:]
    own, _, ends = plan(scalars)
    group = query.shape[1] // HEAD_WIDTH
    for ref in (out, grad_query, local_key, local_value, key_part, value_part):
        ref[...] = jnp.zeros(ref.shape, ref.dtype)

    def put(tile, row, out_tile, grad_query_tile, top, inverse, row_dot):
        put_tile(out, row, group, out_tile)
        put_tile(grad_query, row, group, grad_query_tile)

    segment(
        own, 0, ends,
        lambda row: tile_of(query, row, group), lambda row: tile_of(grad, row, group),
        keys[...], values[...], local_keys[...], local_values[...],
        group, put, key_part, value_part, local_key, local_value,
    )


def left_kernel(*refs):
    scalars = refs[:5]
    (rows, keys, values, local_keys, local_values,
     left_out, left_grad_query, key_acc, value_acc, stats) = refs[5:]
    own, total, ends = plan(scalars)
    count = total - own
    heads = range(keys.shape[1] // HEAD_WIDTH)
    width = rows.shape[2] // len(heads)
    group = width // HEAD_WIDTH
    columns = group * TILE_ROWS
    all_rows = left_out.shape[0]
    for ref in (left_out, left_grad_query, key_acc, value_acc, stats):
        ref[...] = jnp.zeros(ref.shape, ref.dtype)

    scale2 = SCORE_SCALE * LOG2_E
    parts = chunks(keys.shape[0], KEY_CHUNK)

    def head_columns(head):
        return slice(head * HEAD_WIDTH, (head + 1) * HEAD_WIDTH)

    def body(tile, carry):
        row = pl.multiple_of(tile * TILE_ROWS, TILE_ROWS)
        queries = [tile_of(rows.at[0], row, group, head * width) for head in heads]
        grads = [tile_of(rows.at[1], row, group, head * width) for head in heads]
        within = row + lax.rem(lax.broadcasted_iota(jnp.int32, (columns, 1), 0), TILE_ROWS)
        place = within + own
        start = jnp.zeros((columns, 1), jnp.int32)
        for end in ends:
            start = jnp.where(place >= end, end, start)
        key = lax.broadcasted_iota(jnp.int32, (columns, all_rows), 1)
        allowed = (key >= start) & (key <= place)
        key_parts = [
            [keys[part, head_columns(head)] for part in parts] + [local_keys[:, head_columns(head)]]
            for head in heads
        ]
        value_parts = [
            [values[part, head_columns(head)] for part in parts] + [local_values[:, head_columns(head)]]
            for head in heads
        ]
        weights, tops, inverses = [], [], []
        for head in heads:
            scores = [dot_nt(queries[head], part) * scale2 for part in key_parts[head]]
            scores[-1] = jnp.where(allowed, scores[-1], NEGATIVE)
            top = functools.reduce(
                jnp.maximum, [jnp.max(score, axis=1, keepdims=True) for score in scores]
            )
            exponents = [jnp.exp2(score - top) for score in scores]
            inverse = 1.0 / sum(jnp.sum(part, axis=1, keepdims=True) for part in exponents)
            weights.append([part * inverse for part in exponents])
            tops.append(top)
            inverses.append(inverse)
        low = [[weight.astype(BF16) for weight in weights[head]] for head in heads]
        lane = lax.broadcasted_iota(jnp.int32, (columns, HEAD_WIDTH), 1)
        where = pl.ds(pl.multiple_of(tile * columns, columns), columns)
        for head in heads:
            result = sum(dot(weight, value) for weight, value in zip(low[head], value_parts[head]))
            result = jnp.where(within < count, result, 0.0).astype(BF16)
            row_dot = jnp.sum(
                result.astype(F32) * grads[head].astype(F32), axis=1, keepdims=True
            )
            grad_scores = [
                (weight * (dot_nt(grads[head], value) - row_dot)).astype(BF16)
                for weight, value in zip(weights[head], value_parts[head])
            ]
            grad_rows = sum(dot(score, part) for score, part in zip(grad_scores, key_parts[head]))
            put_tile(left_out, row, group, result, head * width)
            put_tile(left_grad_query, row, group, (grad_rows * SCORE_SCALE).astype(BF16), head * width)
            key_acc[:, head_columns(head)] += dot(grad_scores[-1].T, queries[head]) * SCORE_SCALE
            value_acc[:, head_columns(head)] += dot(low[head][-1].T, grads[head])
            packed = jnp.where(lane == 0, tops[head], jnp.where(lane == 1, inverses[head], row_dot)).T
            stats[head * 4 : (head + 1) * 4, where] = packed[:4]
        return carry

    lax.fori_loop(0, lax.div(count + TILE_ROWS - 1, TILE_ROWS), body, 0)


def merge_kernel(*refs):
    scalars = refs[:5]
    owns, lefts, outs = refs[5:9], refs[9:13], refs[-4:]
    own, _, _ = plan(scalars)
    rows = outs[0].shape[0]
    target = lax.broadcasted_iota(jnp.int32, (rows, rows), 0)
    source = lax.broadcasted_iota(jnp.int32, (rows, rows), 1)
    place = (target == source + own).astype(BF16)
    for own_rows, left, out in zip(owns[:2], lefts[:2], outs[:2]):
        out[...] = (own_rows[...].astype(F32) + dot(place, left[...])).astype(BF16)
    for own_part, left, out in zip(owns[2:], lefts[2:], outs[2:]):
        out[...] = (own_part[...] + left[...]).astype(BF16)


def arrived_kernel(counts, first, second, stats, keys, values, own_key, own_value, *rest):
    key_out, value_out, key_acc, value_acc = rest[-4:]
    count = counts[1]
    heads = range(keys.shape[1] // HEAD_WIDTH)
    width = first.shape[2] // len(heads)
    group = width // HEAD_WIDTH
    columns = group * TILE_ROWS
    scale2 = SCORE_SCALE * LOG2_E
    key_acc[...] = own_key[...]
    value_acc[...] = own_value[...]
    parts = chunks(keys.shape[0], ARRIVED_CHUNK)
    tiles = lax.div(count + TILE_ROWS - 1, TILE_ROWS)
    full = first.shape[1] // TILE_ROWS

    def steps(rows, first_tile):
        def body(tile, carry):
            row = pl.multiple_of(tile * TILE_ROWS, TILE_ROWS)
            within = first_tile * TILE_ROWS + row + lax.rem(
                lax.broadcasted_iota(jnp.int32, (columns, 1), 0), TILE_ROWS
            )
            where = pl.ds(pl.multiple_of((first_tile + tile) * columns, columns), columns)
            queries, grads = [
                [tile_of(rows.at[index], row, group, head * width) for head in heads]
                for index in range(2)
            ]
            if first_tile:
                queries, grads = [
                    [jnp.where(within < count, tile, 0) for tile in tiles]
                    for tiles in (queries, grads)
                ]
            for part in parts:
                for head in heads:
                    here = slice(head * HEAD_WIDTH, (head + 1) * HEAD_WIDTH)
                    stat = stats[head * 4 : (head + 1) * 4, where]
                    weight = jnp.exp2(
                        dot_nt(keys[part, here], queries[head]) * scale2 - stat[0:1]
                    ) * stat[1:2]
                    grad_scores = (
                        weight * (dot_nt(values[part, here], grads[head]) - stat[2:3])
                    ).astype(BF16)
                    key_acc[part, here] += dot(grad_scores, queries[head])
                    value_acc[part, here] += dot(weight.astype(BF16), grads[head])
            return carry

        return body

    lax.fori_loop(0, jnp.minimum(tiles, full), steps(first, 0), 0)
    lax.fori_loop(0, jnp.maximum(tiles - full, 0), steps(second, full), 0)
    key_out[0] = (key_acc[...] * SCORE_SCALE).astype(BF16)
    value_out[0] = value_acc[...].astype(BF16)


def after(values, others):
    count = len(values)
    return pl.pallas_call(
        lambda *refs: None,
        in_specs=[pl.BlockSpec(memory_space=pl.ANY)] * (count + len(others)),
        out_specs=[pl.BlockSpec(memory_space=pl.ANY)] * count,
        out_shape=[jax.ShapeDtypeStruct(value.shape, value.dtype) for value in values],
        input_output_aliases={k: k for k in range(count)},
        name="after",
    )(*values, *others)


def send_late(late, send_count, receive_count, device):
    devices = lax.axis_size("dp")
    half = late.shape[1]
    if devices % 2:
        return shifted(late, "dp", -1)
    sizes = [size for size in (0, 8, 16, 32) if size < half] + [half]
    even = lax.rem(device, 2) == 0

    def branch(pairs, receives, size):
        def send(value, received):
            if size == 0:
                return received
            got = lax.ppermute(value[:, :size], "dp", pairs)
            got = jnp.where(receives, got, received[:, :size])
            return lax.dynamic_update_slice(received, got, (0, 0, 0))

        return send

    received = late
    for parity in range(2):
        pairs = [(b, (b - 1) % devices) for b in range(parity, devices, 2)]
        sends = even == (parity == 0)
        count = jnp.where(sends, send_count, receive_count)
        choice = sum((count > half + size).astype(jnp.int32) for size in sizes[:-1])
        branches = [branch(pairs, jnp.logical_not(sends), size) for size in sizes]
        received = lax.switch(choice, branches, late, received)
    return received


def per_device(
    queries, response_key_rows, response_value_rows, shared_prompt_keys, shared_prompt_values,
    grad_out, lengths, packing, prompt_of, prompt_owner,
):
    rows = queries.shape[0]
    kv_heads = response_key_rows.shape[1] // HEAD_WIDTH
    width = queries.shape[1] // kv_heads
    prompt = shared_prompt_keys.shape[1]
    device = lax.axis_index("dp").astype(jnp.int32).reshape(1)
    scalars = (device, packing, lengths, prompt_of, prompt_owner)
    smem = [pl.BlockSpec(memory_space=pltpu.SMEM)] * 5
    params = pltpu.CompilerParams(vmem_limit_bytes=VMEM_LIMIT)
    cost = pl.CostEstimate(flops=1, bytes_accessed=1, transcendentals=0)
    shape = jax.ShapeDtypeStruct
    wide = pl.BlockSpec((rows, width), lambda h: (0, h))
    narrow = pl.BlockSpec((rows, HEAD_WIDTH), lambda h: (0, h))
    context = pl.BlockSpec((prompt, HEAD_WIDTH), lambda h: (0, h))
    pair = pl.BlockSpec((2, rows, width), lambda h: (0, 0, h))
    own_keys = shared_prompt_keys[0]
    own_values = shared_prompt_values[0]
    stat_columns = rows * width // HEAD_WIDTH

    left_keys = shifted(own_keys, "dp", 1)
    left_values = shifted(own_values, "dp", 1)

    half = rows // 2
    moved, early, late, counts = pl.pallas_call(
        gather_kernel,
        grid=(1,),
        in_specs=smem + [pl.BlockSpec(queries.shape, lambda i: (0, 0))] * 2,
        out_specs=[
            pl.BlockSpec((2, rows, queries.shape[1]), lambda i: (0, 0, 0)),
            pl.BlockSpec((2, half, queries.shape[1]), lambda i: (0, 0, 0)),
            pl.BlockSpec((2, half, queries.shape[1]), lambda i: (0, 0, 0)),
            pl.BlockSpec(memory_space=pltpu.SMEM),
        ],
        out_shape=[
            shape((2, rows, queries.shape[1]), BF16),
            shape((2, half, queries.shape[1]), BF16), shape((2, half, queries.shape[1]), BF16),
            shape((2,), jnp.int32),
        ],
        compiler_params=params,
        cost_estimate=cost,
        name="gather_rows",
    )(*scalars, queries, grad_out)

    own_out, own_grad_query, own_local_key, own_local_value, own_key, own_value = pl.pallas_call(
        own_kernel,
        grid=(kv_heads,),
        in_specs=smem + [wide, wide, context, context, narrow, narrow],
        out_specs=[wide, wide, narrow, narrow, context, context],
        out_shape=[
            shape(queries.shape, BF16), shape(queries.shape, BF16),
            shape(response_key_rows.shape, F32), shape(response_key_rows.shape, F32),
            shape(own_keys.shape, F32), shape(own_keys.shape, F32),
        ],
        compiler_params=params,
        cost_estimate=cost,
        name="own_rows",
    )(*scalars, queries, grad_out, own_keys, own_values, response_key_rows, response_value_rows)

    both = kv_heads // 2
    context_both = pl.BlockSpec((prompt, both * HEAD_WIDTH), lambda h: (0, h))

    wide_both = pl.BlockSpec((rows, both * width), lambda h: (0, h))
    narrow_both = pl.BlockSpec((rows, both * HEAD_WIDTH), lambda h: (0, h))
    pair_both = pl.BlockSpec((2, rows, both * width), lambda h: (0, 0, h))
    early, left_values = after((early, left_values), (left_keys, own_out))
    left_out, left_grad_query, left_local_key, left_local_value, stats = pl.pallas_call(
        left_kernel,
        grid=(2,),
        in_specs=smem + [pair_both, context_both, context_both, narrow_both, narrow_both],
        out_specs=[
            wide_both, wide_both, narrow_both, narrow_both,
            pl.BlockSpec((4 * both, stat_columns), lambda h: (h, 0)),
        ],
        out_shape=[
            shape(queries.shape, BF16), shape(queries.shape, BF16),
            shape(response_key_rows.shape, F32), shape(response_key_rows.shape, F32),
            shape((4 * kv_heads, stat_columns), F32),
        ],
        compiler_params=params,
        cost_estimate=cost,
        name="left_rows",
    )(*scalars, moved, left_keys, left_values, response_key_rows, response_value_rows)

    out, grad_query, local_key, local_value = pl.pallas_call(
        merge_kernel,
        grid=(kv_heads,),
        in_specs=smem + [wide, wide, narrow, narrow] * 2,
        out_specs=[wide, wide, narrow, narrow],
        out_shape=[
            shape(queries.shape, BF16), shape(queries.shape, BF16),
            shape(response_key_rows.shape, BF16), shape(response_key_rows.shape, BF16),
        ],
        compiler_params=params,
        cost_estimate=cost,
        name="merge_rows",
    )(*scalars, own_out, own_grad_query, own_local_key, own_local_value,
      left_out, left_grad_query, left_local_key, left_local_value)

    (late,) = after((late,), (out,))
    arrived_second = send_late(late, counts[0], counts[1], device[0])
    half_rows = pl.BlockSpec((2, half, both * width), lambda h: (0, 0, h))
    whole = pl.BlockSpec((1, prompt, both * HEAD_WIDTH), lambda h: (0, 0, h))
    prompt_key, prompt_value = pl.pallas_call(
        arrived_kernel,
        grid=(2,),
        in_specs=[
            pl.BlockSpec(memory_space=pltpu.SMEM), half_rows, half_rows,
            pl.BlockSpec((4 * both, stat_columns), lambda h: (h, 0)),
        ] + [context_both] * 4,
        out_specs=[whole, whole],
        out_shape=[shape((1,) + own_keys.shape, BF16)] * 2,
        scratch_shapes=[pltpu.VMEM((prompt, both * HEAD_WIDTH), F32)] * 2,
        compiler_params=params,
        cost_estimate=cost,
        name="arrived_rows",
    )(counts, shifted(early, "dp", -1), arrived_second, shifted(stats, "dp", -1),
      own_keys, own_values, own_key, own_value)
    return out, grad_query, local_key, local_value, prompt_key, prompt_value


def solution(mesh):
    rows = P(("groups", "dp"), "tensor")
    prompts = P(("groups", "dp"), None, "tensor")
    in_specs = (
        rows, rows, rows, prompts, prompts, rows,
        P("groups"), P(("groups", "dp"), None), P("groups"), P("groups"),
    )
    out_specs = (rows, rows, rows, rows, prompts, prompts)
    return jax.shard_map(
        per_device, mesh=mesh, in_specs=in_specs, out_specs=out_specs, check_vma=False
    )
```
